256 devices in a mesh: seq: 64 (over z, x, core), head: 4 (over y).
Axes of the slice: x: 4, y: 4, z: 8, core: 2. Of those that a mesh axis runs over, the one named last changes fastest.
Arguments:
- queries: bfloat16 [73728, 32, 128], P(('seq', 'head')), may hold values from -4 to 4
- key_states: bfloat16 [73728, 4, 128], P(('seq', 'head')), may hold values from -4 to 4
- value_states: bfloat16 [73728, 4, 128], P(('seq', 'head')), may hold values from -6 to 6
- outputs: bfloat16 [73728, 32, 128], P(('seq', 'head')), may hold values from -6 to 6
- output_grad: bfloat16 [73728, 32, 128], P(('seq', 'head')), may hold values from -96 to 96
- logsumexp: float32 [73728, 32], P(('seq', 'head')), may hold values from 6.8 to 7.8
- random_owner: int32 [576, 3], replicated, may hold values from 0 to 63, all different within a row; in each aligned block of 9 rows (0 to 8, 9 to 17, ...) no two rows name the same one
- random_slot: int32 [576, 3], replicated, may hold values from 0 to 8
Outputs:
- query_grad: bfloat16 [73728, 32, 128], P(('seq', 'head'))
- key_grad: bfloat16 [73728, 4, 128], P(('seq', 'head'))
- value_grad: bfloat16 [73728, 4, 128], P(('seq', 'head'))
The draws below stay inside these ranges and needn't reach their ends.
Inputs may be any that keep to these rules, and one draw needn't show every extreme that they name: `random_owner`: each row names 3 different indices. Within the 9 rows of one index of seq (aligned blocks of 9 rows), no index of seq appears more than 1 times, and some index appears exactly 1 times in some block.
All inputs are finite; a program needn't handle non-finite values.
Results may differ from the reference program's by a relative error of at most 0.005.
Values may be sent and summed in bfloat16 or wider, within the bound.
No kernel may reach another device: no remote copies, remote signals or barrier semaphores. Data moves between devices by JAX's collectives and lax.ppermute only.
A program may use at most 128 MiB of HBM per device.

```python
import math
import jax
import jax.numpy as jnp
import numpy as np
from jax import lax

QH = 32
KVH = 4
HD = 128
BLK = 128
G = 2
RND = 3
TOKENS = 73728
NB = 576
QB = 9
MOST = 1
N_SEQ = 64


def bounded_field(key, field_shape):
    return jnp.clip(jax.random.normal(key, field_shape, jnp.float32), -4.0, 4.0)


def draw_queries(key, part):
    return bounded_field(jax.random.fold_in(key, 11), (TOKENS, QH, HD)).astype(jnp.bfloat16)


def draw_key_states(key, part):
    return bounded_field(jax.random.fold_in(key, 23), (TOKENS, KVH, HD)).astype(jnp.bfloat16)


def set_ends(array, own_key, smallest, top_value):
    extent = array.shape
    spot = [jax.random.randint(jax.random.fold_in(own_key, axis), (), 0, extent[axis]) for axis in range(len(extent))]
    array = array.at[tuple(spot)].set(smallest)
    longest = extent.index(max(extent))
    spot[longest] = (spot[longest] + 1) % extent[longest]
    return array.at[tuple(spot)].set(top_value)


def block_levels(own_key, dims, cuts, smallest, high):
    level = 1.0
    for dim, blocks in cuts:
        draws = jax.random.uniform(jax.random.fold_in(jax.random.fold_in(own_key, 6), dim), (blocks,), jnp.float32, smallest / len(cuts), high / len(cuts))
        level = level * jnp.repeat(jnp.exp(draws), dims[dim] // blocks).reshape((-1,) + (1,) * (len(dims) - 1 - dim))
    return level


def shared_out(stream_key, own, number, rows, amount, top, most, lean):
    ranking = jax.random.permutation(stream_key, amount)
    heavy_load, ordinary = load_shares(amount, rows * top, most, lean, True), load_shares(amount, rows * top, most, lean, False)
    places = jnp.arange(amount)

    def named(tallies, offset_by):
        used = int((tallies > 0).sum())
        fixed = max(1, used // 4)
        passed = fixed + (places - fixed + offset_by * (used - fixed)) % max(1, amount - fixed)
        return jnp.zeros((amount,), jnp.int32).at[ranking[jnp.where(places < fixed, places, passed)]].set(jnp.asarray(tallies, jnp.int32))

    tallies = jnp.where(number % 4 == 0, named(heavy_load, number // 4), named(ordinary, number - number // 4 - 1))
    mixed = jax.random.permutation(jax.random.fold_in(own, 3), amount)
    donor, sink = mixed[0:amount // 2 * 2:2], mixed[1:amount // 2 * 2:2]
    slack = jnp.minimum(tallies[donor] - 1, most - tallies[sink]) // 2
    slack = jnp.where((donor == ranking[0]) | (sink == ranking[0]) | (tallies[sink] == 0), 0, jnp.maximum(slack, 0))
    passed = jax.random.randint(jax.random.fold_in(own, 4), (amount // 2,), 0, 1 << 20) % (slack + 1)
    tallies = tallies.at[donor].add(-passed).at[sink].add(passed)
    members = jnp.searchsorted(jnp.cumsum(tallies), jnp.arange(rows * top), side="right").astype(jnp.int32)
    grid = members.reshape(top, rows).T
    grid = grid[jax.random.permutation(jax.random.fold_in(own, 1), rows)]
    offset_by = jax.random.randint(jax.random.fold_in(own, 2), (rows, 1), 0, top)
    return jnp.take_along_axis(grid, (jnp.arange(top)[None, :] + offset_by) % top, axis=1)


def load_shares(amount, total, reach, slope, full):
    loads = [(1 << 20) // math.isqrt(standing ** slope) + 1 for standing in range(1, amount + 1)]
    largest = reach if full else min(reach, max(-(-total // amount), total * loads[0] // sum(loads)))
    least = 1 if total - largest >= amount - 1 else 0
    counts, spare = [largest] + [least] * (amount - 1), total - largest - least * (amount - 1)
    while spare > 0:
        free = [i for i in range(1, amount) if counts[i] < largest] or [i for i in range(1, amount) if counts[i] < reach]
        mass, left = sum([loads[i] for i in free]), spare
        for i in free:
            addition = min(reach - counts[i], max(1, left * loads[i] // mass), spare)
            counts[i] = counts[i] + addition
            spare = spare - addition
    return np.array(counts)


def noise(own_key, shape, deviation, bound, pieces=(), kind=jnp.bfloat16):
    result = jax.random.normal(own_key, shape, jnp.float32) * deviation
    if len(pieces) > 0:
        result = block_levels(own_key, shape, pieces, -0.22, 0.18) * result
    return jnp.clip(result, min=-bound, max=bound).astype(kind)


def setup_inputs(seed: int = 0) -> dict:
    seeds = jax.random.split(jax.random.key(seed), 9)
    queries = draw_queries(jax.random.fold_in(seeds[8], 71), 0)
    key_states = draw_key_states(jax.random.fold_in(seeds[8], 71), 0)
    value_states = noise(seeds[2], (TOKENS, KVH, HD), 1.0, 6.0, ((0, 256),))
    outputs = noise(seeds[3], (TOKENS, QH, HD), 1.0, 6.0, ((0, 256),))
    output_grad = noise(seeds[4], (TOKENS, QH, HD), 16.0, 96.0, ((0, 256),))
    logsumexp = jnp.clip(6.8 + 1.0 * jax.random.uniform(seeds[5], (TOKENS, QH), jnp.float32) ** block_levels(seeds[5], (TOKENS, QH), ((0, 256),), -0.2, 0.2), 6.8, 7.8)
    random_owner_keys = jax.random.split(jax.random.fold_in(seeds[6], 1), NB // QB)
    random_owner_turns = jax.random.permutation(jax.random.fold_in(seeds[6], 3), NB // QB)
    random_owner = jax.vmap(lambda own, number: shared_out(jax.random.fold_in(seeds[6], 2), own, number, QB, N_SEQ, RND, MOST, 2))(random_owner_keys, random_owner_turns).reshape((NB, RND))
    random_slot = set_ends(jax.random.randint(seeds[7], (NB, RND), 0, QB), jax.random.fold_in(seeds[7], 1), 0, QB - 1).astype(jnp.int32)
    return dict(queries=queries, key_states=key_states, value_states=value_states, outputs=outputs, output_grad=output_grad, logsumexp=logsumexp, random_owner=random_owner, random_slot=random_slot)


def narrow_value(values):
    return lax.optimization_barrier(values.astype(jnp.bfloat16)).astype(values.dtype)


def block_lists(block_id, random_owner, random_slot):
    global_ids = jnp.arange(G, dtype=jnp.int32)
    window_ids = block_id + jnp.arange(-1, 2, dtype=jnp.int32)
    random_ids = (random_owner[block_id] * QB + random_slot[block_id]).astype(jnp.int32)
    window_ok = (window_ids >= G) & (window_ids <= NB - 1)
    random_ok = (random_ids >= G) & (jnp.abs(random_ids - block_id) >= 2)
    validity = jnp.concatenate([jnp.ones((G,), jnp.float32), window_ok.astype(jnp.float32), random_ok.astype(jnp.float32)])
    indices = jnp.clip(jnp.concatenate([global_ids, window_ids, random_ids]), 0, NB - 1).astype(jnp.int32)
    return indices, validity


def block_grads(query_block, grad_block, logsum_block, delta_block, key_blocks, value_blocks, validity):
    scaling = 1.0 / (HD ** 0.5)
    scores = jnp.einsum("ighd,mjgd->mghij", query_block, key_blocks) * scaling
    weights = jnp.exp(scores - jnp.transpose(logsum_block, (1, 2, 0))[None, :, :, :, None]) * validity[:, None, None, None, None]
    weights_rounded = narrow_value(weights)
    weight_grad = jnp.einsum("ighd,mjgd->mghij", grad_block, value_blocks)
    score_grad = narrow_value(weights * (weight_grad - jnp.transpose(delta_block, (1, 2, 0))[None, :, :, :, None]))
    query_part = jnp.einsum("mghij,mjgd->ighd", score_grad, key_blocks) * scaling
    key_part = jnp.einsum("mghij,ighd->mjgd", score_grad, query_block) * scaling
    value_part = jnp.einsum("mghij,ighd->mjgd", weights_rounded, grad_block)
    return query_part, jnp.stack([key_part, value_part], axis=2)


def reference(queries, key_states, value_states, outputs, output_grad, logsumexp, random_owner, random_slot):
    group = QH // KVH
    query_full = queries.astype(jnp.float32).reshape(NB, BLK, KVH, group, HD)
    grad_full = output_grad.astype(jnp.float32).reshape(NB, BLK, KVH, group, HD)
    row_delta = jnp.sum(output_grad.astype(jnp.float32) * outputs.astype(jnp.float32), axis=-1)
    delta_blocks = row_delta.reshape(NB, BLK, KVH, group)
    logsum_blocks = logsumexp.reshape(NB, BLK, KVH, group)
    kv_blocks = jnp.stack([key_states, value_states], axis=1).astype(jnp.float32).reshape(NB, BLK, 2, KVH, HD)

    def advance(carry, block_id):
        indices, validity = block_lists(block_id, random_owner, random_slot)
        chosen = kv_blocks[indices]
        query_part, kv_part = block_grads(query_full[block_id], grad_full[block_id], logsum_blocks[block_id], delta_blocks[block_id], chosen[:, :, 0], chosen[:, :, 1], validity)
        carry = carry.at[indices].add(kv_part)
        return carry, query_part

    initial = jnp.zeros((NB, BLK, 2, KVH, HD), jnp.float32)
    kv_grad, query_parts = lax.scan(advance, initial, jnp.arange(NB, dtype=jnp.int32))
    query_grad = query_parts.reshape(TOKENS, QH, HD).astype(jnp.bfloat16)
    key_grad = kv_grad[:, :, 0].reshape(TOKENS, KVH, HD).astype(jnp.bfloat16)
    value_grad = kv_grad[:, :, 1].reshape(TOKENS, KVH, HD).astype(jnp.bfloat16)
    return (query_grad, key_grad, value_grad)
```

```python
import functools

import jax
import jax.numpy as jnp
import numpy as np
from jax import lax
from jax.experimental import pallas as pl
from jax.experimental.pallas import tpu as pltpu
from jax.sharding import Mesh, PartitionSpec as P

HD = 128
BLK = 128
G = 2
RND = 3
NZ, NX, NC, NH = 8, 4, 2, 4
NXC = NX * NC
SEQ = ("z", "x", "c")
NSEQ = NZ * NXC
QB = 9
NB = NSEQ * QB
HL = 8
ROWS = BLK * HL
TOK = 288
SCALE = 1.0 / HD**0.5
LOG2E = 1.4426950408889634
MASKED = 1e30
ENT = NB * RND
AT_SEQ, AT_Z, AT_HEAD, AT_WANT = 2 * ENT, 2 * ENT + 1, 2 * ENT + 2, 2 * ENT + 3
NEAR, FAR = (0, 1, 2, 6, 7), (3, 4, 5)
CUT = 5
PART = TOK * HL
BF = jnp.bfloat16
F32 = jnp.float32
ANY = pl.ANY


def dot(a, b, ca, cb):
    return lax.dot_general(a, b, (((ca,), (cb,)), ((), ())), preferred_element_type=F32)


def row_vector(tile):
    return jnp.concatenate([tile[i : i + 1, :] for i in range(HL)], axis=1)


def pair_grads(keys, values, biases, q, do, lse2, delta, key_scr, p_scr, ds_scr):
    n = len(keys)
    for t in range(n):
        rows = pl.ds(t * BLK, BLK)
        key_scr[rows, :] = keys[t]
        s = dot(keys[t], q, 1, 1)
        p = jnp.exp2(s * (SCALE * LOG2E) - (lse2 + biases[t]))
        dp = dot(values[t], do, 1, 1)
        p_scr[rows, :] = p.astype(BF)
        ds_scr[rows, :] = (p * (dp - delta)).astype(BF)
    dv = dot(p_scr[...], do, 1, 0)
    dk = dot(ds_scr[...], q, 1, 0) * SCALE
    dqt = dot(key_scr[...], ds_scr[...], 0, 0)
    return dk, dv, dqt


def load_parts(meta, parts, whole, sems):
    copies = []
    for i, (four, target) in enumerate(zip(parts, whole)):
        for k in range(NH):
            row = pl.multiple_of(((meta[AT_HEAD] - k) & (NH - 1)) * PART, PART)
            copies.append(
                pltpu.make_async_copy(four[k], target.at[pl.ds(row, PART)], sems.at[i, k])
            )
    for c in copies:
        c.start()
    for c in copies:
        c.wait()


def near_kernel(
    meta, q0, q1, q2, q3, d0, d1, d2, d3, ld_ref, kv_ref, gl_ref,
    dqt_ref, dkv_ref, dg_ref, q_scr, do_scr, key_scr, p_scr, ds_scr, sems,
):
    b = pl.program_id(0)

    @pl.when(b == 0)
    def _():
        load_parts(meta, ((q0, q1, q2, q3), (d0, d1, d2, d3)), (q_scr, do_scr), sems)
        dkv_ref[...] = jnp.zeros_like(dkv_ref)
        dg_ref[...] = jnp.zeros_like(dg_ref)

    block = meta[AT_SEQ] * QB + b
    keys = [gl_ref[0, 0], gl_ref[1, 0]] + [kv_ref[b + w, 0] for w in range(3)]
    values = [gl_ref[0, 1], gl_ref[1, 1]] + [kv_ref[b + w, 1] for w in range(3)]
    biases = [0.0, 0.0]
    for w in range(3):
        c = block + (w - 1)
        biases.append(jnp.where((c >= G) & (c <= NB - 1), 0.0, MASKED))
    lse2, delta = row_vector(ld_ref[0, 0]), row_vector(ld_ref[1, 0])
    rows = pl.ds(pl.multiple_of(b * ROWS, ROWS), ROWS)
    dk, dv, dqt = pair_grads(
        keys, values, biases, q_scr[rows, :], do_scr[rows, :], lse2, delta, key_scr, p_scr, ds_scr
    )
    dqt_ref[0] = dqt
    for t in range(G):
        dg_ref[t, 0] += dk[t * BLK : (t + 1) * BLK]
        dg_ref[t, 1] += dv[t * BLK : (t + 1) * BLK]
    for w in range(3):
        t = G + w
        dkv_ref[b + w, 0] += dk[t * BLK : (t + 1) * BLK]
        dkv_ref[b + w, 1] += dv[t * BLK : (t + 1) * BLK]


def place_of(meta, owner):
    r = ((owner >> 3) - meta[AT_Z]) & (NZ - 1)
    source = owner & (NXC - 1)
    far = (r >= FAR[0]) & (r <= FAR[-1])
    pos = jnp.where(r >= FAR[0], r - FAR[0], r)
    return far, source * jnp.where(far, len(FAR), len(NEAR)) + pos


def random_kernel(
    meta, q0, q1, q2, q3, d0, d1, d2, d3, ld_ref, near_ref, far_ref, dqt_ref,
    dq0, dq1, dq2, dq3, dnear_ref, dfar_ref,
    q_scr, do_scr, dq_scr, kv_scr, out_scr, key_scr, p_scr, ds_scr, sems, in_sems, out_sems, dq_sems,
):
    b = pl.program_id(0)
    start = meta[AT_SEQ] * (QB * RND)

    @pl.when(b == 0)
    def _():
        for e in range(QB * RND):
            far, at = place_of(meta, meta[start + e])

            @pl.when(far)
            def _():
                pltpu.make_async_copy(far_ref.at[at], kv_scr.at[e], in_sems.at[e]).start()

            @pl.when(jnp.logical_not(far))
            def _():
                pltpu.make_async_copy(near_ref.at[at], kv_scr.at[e], in_sems.at[e]).start()

        load_parts(meta, ((q0, q1, q2, q3), (d0, d1, d2, d3)), (q_scr, do_scr), sems)

    first = b * RND
    block = meta[AT_SEQ] * QB + b
    biases = []
    for j in range(RND):
        o = meta[start + first + j]
        r = o * QB + meta[ENT + start + first + j]
        biases.append(jnp.where((r >= G) & (jnp.abs(r - block) >= 2), 0.0, MASKED))
        pltpu.make_async_copy(near_ref.at[0], kv_scr.at[first + j], in_sems.at[first + j]).wait()
    lse2, delta = row_vector(ld_ref[0, 0]), row_vector(ld_ref[1, 0])
    rows = pl.ds(pl.multiple_of(b * ROWS, ROWS), ROWS)
    dk, dv, dqt = pair_grads(
        [kv_scr[first + j, 0] for j in range(RND)],
        [kv_scr[first + j, 1] for j in range(RND)],
        biases, q_scr[rows, :], do_scr[rows, :], lse2, delta, key_scr, p_scr, ds_scr,
    )
    dq_scr[rows, :] = ((dqt + dqt_ref[0]).T * SCALE).astype(BF)

    for j in range(RND):
        n = first + j
        out_scr[n, 0] = dk[j * BLK : (j + 1) * BLK].astype(BF)
        out_scr[n, 1] = dv[j * BLK : (j + 1) * BLK].astype(BF)
        far, at = place_of(meta, meta[start + n])

        @pl.when(far)
        def _():
            pltpu.make_async_copy(out_scr.at[n], dfar_ref.at[at], out_sems.at[n]).start()

        @pl.when(jnp.logical_not(far))
        def _():
            pltpu.make_async_copy(out_scr.at[n], dnear_ref.at[at], out_sems.at[n]).start()

    @pl.when(b == QB - 1)
    def _():
        copies = []
        for k, target in enumerate((dq0, dq1, dq2, dq3)):
            row = pl.multiple_of(((meta[AT_HEAD] + k) & (NH - 1)) * PART, PART)
            copies.append(
                pltpu.make_async_copy(dq_scr.at[pl.ds(row, PART)], target, dq_sems.at[k])
            )
        for c in copies:
            c.start()
        for c in copies:
            c.wait()
        for e in range(QB * RND):
            pltpu.make_async_copy(out_scr.at[e], dnear_ref.at[0], out_sems.at[e]).wait()


def select_kernel(steps, meta, *refs):
    sources, dst = refs[:-1], refs[-1]

    def lay(wanted, src, slot, at):
        @pl.when(wanted)
        def _():
            dst[at] = src[slot]

    for d in range(NXC):
        for i, r in enumerate(steps):
            slot = meta[AT_WANT + d * NZ + r]
            at = d * len(steps) + i
            if r == 4:
                lay((slot >= 0) & (slot < CUT), sources[i], slot, at)
                lay(slot >= CUT, sources[-1], slot - CUT, at)
            else:
                lay(slot >= 0, sources[i], slot, at)


def collect_kernel(steps, meta, got, *outs):
    for out in outs:
        out[...] = jnp.zeros_like(out)
    for d in range(NXC):
        for i, r in enumerate(steps):
            slot = meta[AT_WANT + d * NZ + r]

            @pl.when(slot >= 0)
            def _():
                outs[i][slot] += got[d * len(steps) + i].astype(F32)


TILE = (2, BLK, HD)
PARAMS = pltpu.CompilerParams(vmem_limit_bytes=50 << 20)


def full(*shape):
    return pl.BlockSpec(shape, lambda b, m: (0,) * len(shape))


def anywhere(n):
    return [pl.BlockSpec(memory_space=ANY)] * n


def work_scratch(n):
    return [
        pltpu.VMEM((n * BLK, HD), BF),
        pltpu.VMEM((n * BLK, ROWS), BF),
        pltpu.VMEM((n * BLK, ROWS), BF),
    ]


ROW_PAIR = pl.BlockSpec((2, 1, HL, BLK), lambda b, m: (0, b, 0, 0))
DQT = pl.BlockSpec((1, HD, ROWS), lambda b, m: (b, 0, 0))


def call_near(meta, q, do, ld, kvx, gl):
    return pl.pallas_call(
        near_kernel,
        grid_spec=pltpu.PrefetchScalarGridSpec(
            num_scalar_prefetch=1,
            grid=(QB,),
            in_specs=anywhere(2 * NH) + [ROW_PAIR, full(QB + 2, *TILE), full(G, *TILE)],
            out_specs=[DQT, full(QB + 2, *TILE), full(G, *TILE)],
            scratch_shapes=[pltpu.VMEM((QB * ROWS, HD), BF)] * 2
            + work_scratch(G + 3)
            + [pltpu.SemaphoreType.DMA((2, NH))],
        ),
        out_shape=[
            jax.ShapeDtypeStruct((QB, HD, ROWS), F32),
            jax.ShapeDtypeStruct((QB + 2, *TILE), F32),
            jax.ShapeDtypeStruct((G, *TILE), F32),
        ],
        compiler_params=PARAMS,
        name="near",
    )(meta, *q, *do, ld, kvx, gl)


def call_random(meta, q, do, ld, near, far, dqt):
    count = QB * RND
    return pl.pallas_call(
        random_kernel,
        grid_spec=pltpu.PrefetchScalarGridSpec(
            num_scalar_prefetch=1,
            grid=(QB,),
            in_specs=anywhere(2 * NH) + [ROW_PAIR] + anywhere(2) + [DQT],
            out_specs=anywhere(NH + 2),
            scratch_shapes=[pltpu.VMEM((QB * ROWS, HD), BF)] * 3
            + [pltpu.VMEM((count, *TILE), BF)] * 2
            + work_scratch(RND)
            + [
                pltpu.SemaphoreType.DMA((2, NH)),
                pltpu.SemaphoreType.DMA((count,)),
                pltpu.SemaphoreType.DMA((count,)),
                pltpu.SemaphoreType.DMA((NH,)),
            ],
        ),
        out_shape=[jax.ShapeDtypeStruct((PART, HD), BF)] * NH
        + [
            jax.ShapeDtypeStruct((NXC * len(NEAR), *TILE), BF),
            jax.ShapeDtypeStruct((NXC * len(FAR), *TILE), BF),
        ],
        compiler_params=PARAMS,
        name="random",
    )(meta, *q, *do, ld, near, far, dqt)


def call_select(meta, steps, sources):
    n = NXC * len(steps)
    return pl.pallas_call(
        functools.partial(select_kernel, steps),
        grid_spec=pltpu.PrefetchScalarGridSpec(
            num_scalar_prefetch=1,
            grid=(1,),
            in_specs=[full(*x.shape) for x in sources],
            out_specs=full(n, *TILE),
        ),
        out_shape=jax.ShapeDtypeStruct((n, *TILE), BF),
        compiler_params=PARAMS,
        name="select",
    )(meta, *sources)


def call_collect(meta, steps, got):
    return pl.pallas_call(
        functools.partial(collect_kernel, steps),
        grid_spec=pltpu.PrefetchScalarGridSpec(
            num_scalar_prefetch=1,
            grid=(1,),
            in_specs=[full(*got.shape)],
            out_specs=[full(QB, *TILE)] * len(steps),
        ),
        out_shape=[jax.ShapeDtypeStruct((QB, *TILE), F32)] * len(steps),
        compiler_params=PARAMS,
        name="collect",
    )(meta, got)


def join_kernel(head, p0, p1, p2, p3, out):
    for k, p in enumerate((p0, p1, p2, p3)):
        out[:, (head[0] - k) & (NH - 1)] = p[...]


def call_join(head, parts):
    rows = TOK // 3
    return pl.pallas_call(
        join_kernel,
        grid_spec=pltpu.PrefetchScalarGridSpec(
            num_scalar_prefetch=1,
            grid=(3,),
            in_specs=[pl.BlockSpec((rows, HL, HD), lambda b, m: (b, 0, 0))] * NH,
            out_specs=pl.BlockSpec((rows, NH, HL, HD), lambda b, m: (b, 0, 0, 0)),
        ),
        out_shape=jax.ShapeDtypeStruct((TOK, NH, HL, HD), BF),
        name="join",
    )(head, *[p.reshape(TOK, HL, HD) for p in parts])


def plain_a2a(value, axis):
    return lax.all_to_all(value, axis, split_axis=0, concat_axis=0, tiled=True)


def turn(value, k):
    return lax.ppermute(value, "head", [(i, (i + k) % NH) for i in range(NH)]) if k else value


def to_heads(value, head):
    parts = value.reshape(TOK, NH, HL, HD)
    return [
        turn(
            lax.dynamic_index_in_dim(parts, lax.rem(head + k, NH), axis=1, keepdims=False), k
        ).reshape(PART, HD)
        for k in range(NH)
    ]


def along_z(value, step):
    return lax.ppermute(value, "z", [(i, (i + step) % NZ) for i in range(NZ)])


def add(a, b):
    return (a.astype(F32) + b).astype(BF)


def spread(value, index):
    k = 1
    while k < NSEQ:
        got = lax.ppermute(value, SEQ, [(i, i + k) for i in range(k)])
        value = jnp.where((index >= k) & (index < 2 * k), got, value)
        k *= 2
    return value


def gather_sum(value):
    k = NSEQ // 2
    while k:
        value = value + lax.ppermute(value, SEQ, [(i + k, i) for i in range(k)])
        k //= 2
    return value


def per_device(q, k, v, o, do, lse, owner, slot):
    head, seq = lax.axis_index("head"), lax.axis_index(SEQ)
    z, xc = lax.axis_index("z"), lax.axis_index(("x", "c"))
    plane = NXC * QB
    owners = lax.dynamic_slice_in_dim(owner, z * plane, plane, 0).reshape(NXC, 1, QB * RND)
    slots = lax.dynamic_slice_in_dim(slot, z * plane, plane, 0).reshape(NXC, 1, QB * RND)
    column = ((z + jnp.arange(NZ, dtype=jnp.int32)) % NZ * NXC + xc)[None, :, None]
    want = jnp.max(jnp.where(owners == column, slots, -1), axis=2)
    spot = jnp.stack([seq, z, head]).astype(jnp.int32)
    meta = jnp.concatenate([owner.reshape(-1), slot.reshape(-1), spot, want.reshape(-1)])

    kv = jnp.stack([k, v]).transpose(2, 0, 1, 3)
    kv = plain_a2a(kv, "head")
    kv = kv.transpose(1, 0, 2, 3).reshape(2, QB, BLK, HD).transpose(1, 0, 2, 3)
    u1, d1 = along_z(kv, 1), along_z(kv, -1)
    u2, d2 = along_z(u1, 1), along_z(d1, -1)
    u3, d3 = along_z(u2, 1), along_z(d2, -1)
    u4, d4 = along_z(u3[:CUT], 1), along_z(d3[CUT:], -1)
    near = plain_a2a(call_select(meta, NEAR, [kv, d1, d2, u2, u1]), ("x", "c"))
    far = plain_a2a(call_select(meta, FAR, [d3, u4, u3, d4]), ("x", "c"))

    up = [(i, i + 1) for i in range(NSEQ - 1)]
    down = [(i + 1, i) for i in range(NSEQ - 1)]
    before = lax.ppermute(kv[QB - 1 :], SEQ, up)
    after = lax.ppermute(kv[:1], SEQ, down)
    kvx = jnp.concatenate([before, kv, after])
    gl = spread(kv[:G], seq)

    delta = jnp.sum(do.astype(F32) * o.astype(F32), axis=-1)
    ld = jnp.stack([lse * LOG2E, delta]).reshape(2, TOK, NH, HL).transpose(2, 0, 1, 3)
    ld = plain_a2a(ld.reshape(NH, 2, PART // BLK, BLK), "head")
    ld = ld.transpose(1, 0, 2, 3).reshape(2, QB, HL, BLK)

    ql, dol = to_heads(q, head), to_heads(do, head)
    dqt, dkvx, dg = call_near(meta, ql, dol, ld, kvx, gl)
    dq0, dq1, dq2, dq3, dnear, dfar = call_random(meta, ql, dol, ld, near, far, dqt)

    c3, c4, c5 = call_collect(meta, FAR, plain_a2a(dfar, ("x", "c")))
    c0, c1, c2, c6, c7 = call_collect(meta, NEAR, plain_a2a(dnear, ("x", "c")))
    up4 = along_z(c4[:CUT].astype(BF), 1)
    down4 = along_z(c4[CUT:].astype(BF), -1)
    up3 = along_z(jnp.concatenate([add(up4, c3[:CUT]), c3[CUT:].astype(BF)]), 1)
    down3 = along_z(jnp.concatenate([c5[:CUT].astype(BF), add(down4, c5[CUT:])]), -1)
    up2, down2 = along_z(add(up3, c2), 1), along_z(add(down3, c6), -1)
    up1, down1 = along_z(add(up2, c1), 1), along_z(add(down2, c7), -1)

    lower = lax.ppermute(dkvx[:1].astype(BF), SEQ, down)
    upper = lax.ppermute(dkvx[QB + 1 :].astype(BF), SEQ, up)
    dg = jnp.where(seq == 0, gather_sum(dg), 0.0)
    total = dkvx[1 : QB + 1] + c0 + up1.astype(F32) + down1.astype(F32)
    total = total.at[QB - 1 :].add(lower.astype(F32))
    total = total.at[:1].add(upper.astype(F32))
    total = total.at[:G].add(dg).astype(BF)
    dkv = total.transpose(1, 0, 2, 3).reshape(2, NH, TOK, HD).transpose(1, 0, 2, 3)
    dkv = plain_a2a(dkv, "head")
    dk = dkv[:, 0].transpose(1, 0, 2)
    dv = dkv[:, 1].transpose(1, 0, 2)
    dq = call_join(head.reshape(1), [turn(p, i) for i, p in enumerate((dq0, dq1, dq2, dq3))])
    return dq.reshape(TOK, NH * HL, HD), dk, dv


def solution(mesh):
    grid = Mesh(np.asarray(mesh.devices).reshape(NZ, NX, NC, NH), ("z", "x", "c", "head"))
    split = ("z", "x", "c", "head")
    wide = P(split, None, None)
    return jax.shard_map(
        per_device,
        mesh=grid,
        in_specs=(wide,) * 5 + (P(split, None), P(), P()),
        out_specs=(wide,) * 3,
        check_vma=False,
    )
```

```python
import functools

import jax
import jax.numpy as jnp
import numpy as np
from jax import lax
from jax.experimental import pallas as pl
from jax.experimental.pallas import tpu as pltpu
from jax.sharding import Mesh, PartitionSpec as P

HD = 128
BLK = 128
G = 2
RND = 3
NZ, NX, NC, NH = 8, 4, 2, 4
SEQ = ("z", "x", "c")
NSEQ = NZ * NX * NC
QB = 9
NB = NSEQ * QB
HL = 8
ROWS = BLK * HL
TOK = 288
SCALE = 1.0 / HD**0.5
LOG2E = 1.4426950408889634
MASKED = 1e30
ENT = QB * RND
AT_SEQ, AT_HEAD, AT_WANT = ENT, ENT + 1, ENT + 2
STEP = 8
PART = TOK * HL
BF = jnp.bfloat16
F32 = jnp.float32
ANY = pl.ANY


def dot(a, b, ca, cb):
    return lax.dot_general(a, b, (((ca,), (cb,)), ((), ())), preferred_element_type=F32)


def row_vector(tile):
    return jnp.concatenate([tile[i : i + 1, :] for i in range(HL)], axis=1)


def pair_grads(keys, values, biases, q, do, lse2, delta, key_scr, p_scr, ds_scr):
    n = len(keys)
    for t in range(n):
        rows = pl.ds(t * BLK, BLK)
        key_scr[rows, :] = keys[t]
        s = dot(keys[t], q, 1, 1)
        p = jnp.exp2(s * (SCALE * LOG2E) - (lse2 + biases[t]))
        dp = dot(values[t], do, 1, 1)
        p_scr[rows, :] = p.astype(BF)
        ds_scr[rows, :] = (p * (dp - delta)).astype(BF)
    dv = dot(p_scr[...], do, 1, 0)
    dk = dot(ds_scr[...], q, 1, 0) * SCALE
    dqt = dot(key_scr[...], ds_scr[...], 0, 0)
    return dk, dv, dqt


def load_parts(meta, parts, whole, sems):
    copies = []
    for i, (four, target) in enumerate(zip(parts, whole)):
        for k in range(NH):
            row = pl.multiple_of(((meta[AT_HEAD] - k) & (NH - 1)) * PART, PART)
            copies.append(
                pltpu.make_async_copy(four[k], target.at[pl.ds(row, PART)], sems.at[i, k])
            )
    for c in copies:
        c.start()
    for c in copies:
        c.wait()


def near_kernel(
    meta, q0, q1, q2, q3, d0, d1, d2, d3, ld_ref, kv_ref, gl_ref,
    dqt_ref, dkv_ref, dg_ref, q_scr, do_scr, key_scr, p_scr, ds_scr, sems,
):
    b = pl.program_id(0)

    @pl.when(b == 0)
    def _():
        load_parts(meta, ((q0, q1, q2, q3), (d0, d1, d2, d3)), (q_scr, do_scr), sems)
        dkv_ref[...] = jnp.zeros_like(dkv_ref)
        dg_ref[...] = jnp.zeros_like(dg_ref)

    block = meta[AT_SEQ] * QB + b
    keys = [gl_ref[0, 0], gl_ref[1, 0]] + [kv_ref[b + w, 0] for w in range(3)]
    values = [gl_ref[0, 1], gl_ref[1, 1]] + [kv_ref[b + w, 1] for w in range(3)]
    biases = [0.0, 0.0]
    for w in range(3):
        c = block + (w - 1)
        biases.append(jnp.where((c >= G) & (c <= NB - 1), 0.0, MASKED))
    lse2, delta = row_vector(ld_ref[0, 0]), row_vector(ld_ref[1, 0])
    rows = pl.ds(pl.multiple_of(b * ROWS, ROWS), ROWS)
    dk, dv, dqt = pair_grads(
        keys, values, biases, q_scr[rows, :], do_scr[rows, :], lse2, delta, key_scr, p_scr, ds_scr
    )
    dqt_ref[0] = dqt
    for t in range(G):
        dg_ref[t, 0] += dk[t * BLK : (t + 1) * BLK]
        dg_ref[t, 1] += dv[t * BLK : (t + 1) * BLK]
    for w in range(3):
        t = G + w
        dkv_ref[b + w, 0] += dk[t * BLK : (t + 1) * BLK]
        dkv_ref[b + w, 1] += dv[t * BLK : (t + 1) * BLK]


def random_kernel(
    meta, q0, q1, q2, q3, d0, d1, d2, d3, ld_ref, got_ref, dqt_ref,
    dq0, dq1, dq2, dq3, dkv_ref,
    q_scr, do_scr, dq_scr, kv_scr, out_scr, key_scr, p_scr, ds_scr, sems, in_sems, out_sems, dq_sems,
):
    b = pl.program_id(0)

    def fetch(e):
        return pltpu.make_async_copy(got_ref.at[meta[e] >> 4], kv_scr.at[e], in_sems.at[e])

    def give(e):
        return pltpu.make_async_copy(out_scr.at[e], dkv_ref.at[meta[e] >> 4], out_sems.at[e])

    @pl.when(b == 0)
    def _():
        for e in range(ENT):
            fetch(e).start()
        load_parts(meta, ((q0, q1, q2, q3), (d0, d1, d2, d3)), (q_scr, do_scr), sems)

    first = b * RND
    block = meta[AT_SEQ] * QB + b
    biases = []
    for j in range(RND):
        named = meta[first + j]
        r = (named >> 4) * QB + (named & 15)
        biases.append(jnp.where((r >= G) & (jnp.abs(r - block) >= 2), 0.0, MASKED))
        fetch(first + j).wait()
    lse2, delta = row_vector(ld_ref[0, 0]), row_vector(ld_ref[1, 0])
    rows = pl.ds(pl.multiple_of(b * ROWS, ROWS), ROWS)
    dk, dv, dqt = pair_grads(
        [kv_scr[first + j, 0] for j in range(RND)],
        [kv_scr[first + j, 1] for j in range(RND)],
        biases, q_scr[rows, :], do_scr[rows, :], lse2, delta, key_scr, p_scr, ds_scr,
    )
    dq_scr[rows, :] = ((dqt + dqt_ref[0]).T * SCALE).astype(BF)
    for j in range(RND):
        n = first + j
        out_scr[n, 0] = dk[j * BLK : (j + 1) * BLK].astype(BF)
        out_scr[n, 1] = dv[j * BLK : (j + 1) * BLK].astype(BF)
        give(n).start()

    @pl.when(b == QB - 1)
    def _():
        copies = []
        for k, target in enumerate((dq0, dq1, dq2, dq3)):
            row = pl.multiple_of(((meta[AT_HEAD] + k) & (NH - 1)) * PART, PART)
            copies.append(
                pltpu.make_async_copy(dq_scr.at[pl.ds(row, PART)], target, dq_sems.at[k])
            )
        for c in copies:
            c.start()
        for c in copies:
            c.wait()
        for e in range(ENT):
            give(e).wait()


def select_kernel(meta, kv_ref, out_ref):
    base = pl.program_id(0) * STEP
    for i in range(STEP):
        slot = meta[AT_WANT + base + i]

        @pl.when(slot >= 0)
        def _():
            out_ref[i] = kv_ref[slot]


def collect_kernel(meta, got, ext, lower, upper, dg, out, acc):
    step = pl.program_id(0)

    @pl.when(step == 0)
    def _():
        acc[...] = ext[1 : QB + 1]
        acc[QB - 1] += lower[0].astype(F32)
        acc[0] += upper[0].astype(F32)

        @pl.when(meta[AT_SEQ] == 0)
        def _():
            for t in range(G):
                acc[t] += dg[t]

    for i in range(STEP):
        slot = meta[AT_WANT + step * STEP + i]

        @pl.when(slot >= 0)
        def _():
            acc[slot] += got[i].astype(F32)

    @pl.when(step == NSEQ // STEP - 1)
    def _():
        out[...] = acc[...].astype(BF)


TILE = (2, BLK, HD)
PARAMS = pltpu.CompilerParams(vmem_limit_bytes=50 << 20)


def full(*shape):
    return pl.BlockSpec(shape, lambda b, m: (0,) * len(shape))


def anywhere(n):
    return [pl.BlockSpec(memory_space=ANY)] * n


def work_scratch(n):
    return [
        pltpu.VMEM((n * BLK, HD), BF),
        pltpu.VMEM((n * BLK, ROWS), BF),
        pltpu.VMEM((n * BLK, ROWS), BF),
    ]


ROW_PAIR = pl.BlockSpec((2, 1, HL, BLK), lambda b, m: (0, b, 0, 0))
DQT = pl.BlockSpec((1, HD, ROWS), lambda b, m: (b, 0, 0))


def call_near(meta, q, do, ld, kvx, gl):
    return pl.pallas_call(
        near_kernel,
        grid_spec=pltpu.PrefetchScalarGridSpec(
            num_scalar_prefetch=1,
            grid=(QB,),
            in_specs=anywhere(2 * NH) + [ROW_PAIR, full(QB + 2, *TILE), full(G, *TILE)],
            out_specs=[DQT, full(QB + 2, *TILE), full(G, *TILE)],
            scratch_shapes=[pltpu.VMEM((QB * ROWS, HD), BF)] * 2
            + work_scratch(G + 3)
            + [pltpu.SemaphoreType.DMA((2, NH))],
        ),
        out_shape=[
            jax.ShapeDtypeStruct((QB, HD, ROWS), F32),
            jax.ShapeDtypeStruct((QB + 2, *TILE), F32),
            jax.ShapeDtypeStruct((G, *TILE), F32),
        ],
        compiler_params=PARAMS,
        name="near",
    )(meta, *q, *do, ld, kvx, gl)


def call_random(meta, q, do, ld, got, dqt):
    return pl.pallas_call(
        random_kernel,
        grid_spec=pltpu.PrefetchScalarGridSpec(
            num_scalar_prefetch=1,
            grid=(QB,),
            in_specs=anywhere(2 * NH) + [ROW_PAIR] + anywhere(1) + [DQT],
            out_specs=anywhere(NH + 1),
            scratch_shapes=[pltpu.VMEM((QB * ROWS, HD), BF)] * 3
            + [pltpu.VMEM((ENT, *TILE), BF)] * 2
            + work_scratch(RND)
            + [
                pltpu.SemaphoreType.DMA((2, NH)),
                pltpu.SemaphoreType.DMA((ENT,)),
                pltpu.SemaphoreType.DMA((ENT,)),
                pltpu.SemaphoreType.DMA((NH,)),
            ],
        ),
        out_shape=[jax.ShapeDtypeStruct((PART, HD), BF)] * NH
        + [jax.ShapeDtypeStruct((NSEQ, *TILE), BF)],
        compiler_params=PARAMS,
        name="random",
    )(meta, *q, *do, ld, got, dqt)


STEP_TILES = pl.BlockSpec((STEP, *TILE), lambda b, m: (b, 0, 0, 0))


def call_select(meta, kv):
    return pl.pallas_call(
        select_kernel,
        grid_spec=pltpu.PrefetchScalarGridSpec(
            num_scalar_prefetch=1,
            grid=(NSEQ // STEP,),
            in_specs=[full(QB, *TILE)],
            out_specs=STEP_TILES,
        ),
        out_shape=jax.ShapeDtypeStruct((NSEQ, *TILE), BF),
        compiler_params=PARAMS,
        name="select",
    )(meta, kv)


def call_collect(meta, got, ext, lower, upper, dg):
    return pl.pallas_call(
        collect_kernel,
        grid_spec=pltpu.PrefetchScalarGridSpec(
            num_scalar_prefetch=1,
            grid=(NSEQ // STEP,),
            in_specs=[STEP_TILES, full(QB + 2, *TILE), full(1, *TILE), full(1, *TILE), full(G, *TILE)],
            out_specs=full(QB, *TILE),
            scratch_shapes=[pltpu.VMEM((QB, *TILE), F32)],
        ),
        out_shape=jax.ShapeDtypeStruct((QB, *TILE), BF),
        compiler_params=PARAMS,
        name="collect",
    )(meta, got, ext, lower, upper, dg)


def join_kernel(head, p0, p1, p2, p3, out):
    for k, p in enumerate((p0, p1, p2, p3)):
        out[:, (head[0] - k) & (NH - 1)] = p[...]


def call_join(head, parts):
    rows = TOK // 3
    return pl.pallas_call(
        join_kernel,
        grid_spec=pltpu.PrefetchScalarGridSpec(
            num_scalar_prefetch=1,
            grid=(3,),
            in_specs=[pl.BlockSpec((rows, HL, HD), lambda b, m: (b, 0, 0))] * NH,
            out_specs=pl.BlockSpec((rows, NH, HL, HD), lambda b, m: (b, 0, 0, 0)),
        ),
        out_shape=jax.ShapeDtypeStruct((TOK, NH, HL, HD), BF),
        name="join",
    )(head, *[p.reshape(TOK, HL, HD) for p in parts])


def plain_a2a(value, axis):
    return lax.all_to_all(value, axis, split_axis=0, concat_axis=0, tiled=True)


def turn(value, k):
    return lax.ppermute(value, "head", [(i, (i + k) % NH) for i in range(NH)]) if k else value


def head_parts(value, head):
    parts = value.reshape(TOK, NH, HL, HD)
    return [
        lax.dynamic_index_in_dim(parts, lax.rem(head + k, NH), axis=1, keepdims=False).reshape(PART, HD)
        for k in range(NH)
    ]


def tie(*values):
    return lax.optimization_barrier(values)


def spread(value, index):
    k = 1
    while k < NSEQ:
        got = lax.ppermute(value, SEQ, [(i, i + k) for i in range(k)])
        value = jnp.where((index >= k) & (index < 2 * k), got, value)
        k *= 2
    return value


def gather_sum(value):
    k = NSEQ // 2
    while k:
        value = value + lax.ppermute(value, SEQ, [(i + k, i) for i in range(k)])
        k //= 2
    return value


def per_device(q, k, v, o, do, lse, owner, slot):
    head, seq = lax.axis_index("head"), lax.axis_index(SEQ)
    named = (owner * 16 + slot).reshape(NSEQ, ENT)
    mine = lax.dynamic_index_in_dim(named, seq, 0, keepdims=False)
    want = jnp.max(jnp.where(named >> 4 == seq, named & 15, -1), axis=1)
    meta = jnp.concatenate([mine, jnp.stack([seq, head]).astype(jnp.int32), want])

    kv = jnp.stack([k, v]).transpose(2, 0, 1, 3)
    kv = plain_a2a(kv, "head")
    kv = kv.transpose(1, 0, 2, 3).reshape(2, QB, BLK, HD).transpose(1, 0, 2, 3)
    got = plain_a2a(call_select(meta, kv), SEQ)

    up = [(i, i + 1) for i in range(NSEQ - 1)]
    down = [(i + 1, i) for i in range(NSEQ - 1)]
    qp, dop = head_parts(q, head), head_parts(do, head)
    ql = [turn(p, i) for i, p in enumerate(qp)]
    dol = [turn(p, i) for i, p in enumerate(dop)]
    before = lax.ppermute(kv[QB - 1 :], SEQ, up)
    after = lax.ppermute(kv[:1], SEQ, down)
    kvx = jnp.concatenate([before, kv, after])
    gl = spread(kv[:G], seq)
    delta = jnp.sum(do.astype(F32) * o.astype(F32), axis=-1)
    ld = jnp.stack([lse * LOG2E, delta]).reshape(2, TOK, NH, HL).transpose(2, 0, 1, 3)
    ld = ld.reshape(NH, 2, PART // BLK, BLK)
    ld = jnp.stack([turn(lax.dynamic_index_in_dim(ld, lax.rem(head + i, NH), 0, keepdims=False), i) for i in range(NH)])
    ld = jnp.roll(ld[::-1], head + 1, axis=0)
    ld = ld.transpose(1, 0, 2, 3).reshape(2, QB, HL, BLK)

    dqt, dkvx, dg = call_near(meta, ql, dol, ld, kvx, gl)
    *dq, back = call_random(meta, ql, dol, ld, got, dqt)

    back = plain_a2a(back, SEQ)
    dq = call_join(head.reshape(1), [turn(p, i) for i, p in enumerate(dq)])
    lower = lax.ppermute(dkvx[:1].astype(BF), SEQ, down)
    upper = lax.ppermute(dkvx[QB + 1 :].astype(BF), SEQ, up)
    back, dq = tie(back, dq)
    total = call_collect(meta, back, dkvx, lower, upper, gather_sum(dg))
    dkv = total.transpose(1, 0, 2, 3).reshape(2, NH, TOK, HD).transpose(1, 0, 2, 3)
    dkv = plain_a2a(dkv, "head")
    dk = dkv[:, 0].transpose(1, 0, 2)
    dv = dkv[:, 1].transpose(1, 0, 2)
    return dq.reshape(TOK, NH * HL, HD), dk, dv


def solution(mesh):
    grid = Mesh(np.asarray(mesh.devices).reshape(NZ, NX, NC, NH), ("z", "x", "c", "head"))
    split = ("z", "x", "c", "head")
    wide = P(split, None, None)
    return jax.shard_map(
        per_device,
        mesh=grid,
        in_specs=(wide,) * 5 + (P(split, None), P(), P()),
        out_specs=(wide,) * 3,
        check_vma=False,
    )
```

```python
import functools

import jax
import jax.numpy as jnp
import numpy as np
from jax import lax
from jax.experimental import pallas as pl
from jax.experimental.pallas import tpu as pltpu
from jax.sharding import Mesh, PartitionSpec as P

HD = 128
BLK = 128
G = 2
RND = 3
NZ, NX, NC, NH = 8, 4, 2, 4
SEQ = ("z", "x", "c")
NXC = NX * NC
NSEQ = NZ * NXC
QB = 9
NB = NSEQ * QB
HL = 8
ROWS = BLK * HL
TOK = 288
SCALE = 1.0 / HD**0.5
LOG2E = 1.4426950408889634
MASKED = 1e30
ENT = QB * RND
AT_SEQ, AT_HEAD, AT_WANT = ENT, ENT + 1, ENT + 2
STEP = 8
PART = TOK * HL
BF = jnp.bfloat16
F32 = jnp.float32
ANY = pl.ANY


def dot(a, b, ca, cb):
    return lax.dot_general(a, b, (((ca,), (cb,)), ((), ())), preferred_element_type=F32)


def row_vector(tile):
    return jnp.concatenate([tile[i : i + 1, :] for i in range(HL)], axis=1)


def pair_grads(keys, values, biases, q, do, lse2, delta, key_scr, p_scr, ds_scr):
    n = len(keys)
    for t in range(n):
        rows = pl.ds(t * BLK, BLK)
        key_scr[rows, :] = keys[t]
        s = dot(keys[t], q, 1, 1)
        p = jnp.exp2(s * (SCALE * LOG2E) - (lse2 + biases[t]))
        dp = dot(values[t], do, 1, 1)
        p_scr[rows, :] = p.astype(BF)
        ds_scr[rows, :] = (p * (dp - delta)).astype(BF)
    dv = dot(p_scr[...], do, 1, 0)
    dk = dot(ds_scr[...], q, 1, 0) * SCALE
    dqt = dot(key_scr[...], ds_scr[...], 0, 0)
    return dk, dv, dqt


def load_parts(meta, parts, whole, sems):
    copies = []
    for i, (four, target) in enumerate(zip(parts, whole)):
        for k in range(NH):
            row = pl.multiple_of(((meta[AT_HEAD] - k) & (NH - 1)) * PART, PART)
            copies.append(
                pltpu.make_async_copy(four[k], target.at[pl.ds(row, PART)], sems.at[i, k])
            )
    for c in copies:
        c.start()
    for c in copies:
        c.wait()


def near_kernel(
    meta, q0, q1, q2, q3, d0, d1, d2, d3, ld_ref, kv_ref, gl_ref, dqt_ref,
    dq0, dq1, dq2, dq3, dkv_ref, dg_ref, q_scr, do_scr, dq_scr, key_scr, p_scr, ds_scr, sems, dq_sems,
):
    b = pl.program_id(0)

    @pl.when(b == 0)
    def _():
        load_parts(meta, ((q0, q1, q2, q3), (d0, d1, d2, d3)), (q_scr, do_scr), sems)
        dkv_ref[...] = jnp.zeros_like(dkv_ref)
        dg_ref[...] = jnp.zeros_like(dg_ref)

    block = meta[AT_SEQ] * QB + b
    keys = [gl_ref[0], gl_ref[1]] + [kv_ref[b + w, 0] for w in range(3)]
    values = [gl_ref[G], gl_ref[G + 1]] + [kv_ref[b + w, 1] for w in range(3)]
    biases = [0.0, 0.0]
    for w in range(3):
        c = block + (w - 1)
        biases.append(jnp.where((c >= G) & (c <= NB - 1), 0.0, MASKED))
    lse2, delta = row_vector(ld_ref[0, 0]), row_vector(ld_ref[1, 0])
    rows = pl.ds(pl.multiple_of(b * ROWS, ROWS), ROWS)
    dk, dv, dqt = pair_grads(
        keys, values, biases, q_scr[rows, :], do_scr[rows, :], lse2, delta, key_scr, p_scr, ds_scr
    )
    dq_scr[rows, :] = ((dqt + dqt_ref[0]).T * SCALE).astype(BF)
    for t in range(G):
        dg_ref[t, 0] += dk[t * BLK : (t + 1) * BLK]
        dg_ref[t, 1] += dv[t * BLK : (t + 1) * BLK]
    for w in range(3):
        t = G + w
        dkv_ref[b + w, 0] += dk[t * BLK : (t + 1) * BLK]
        dkv_ref[b + w, 1] += dv[t * BLK : (t + 1) * BLK]

    @pl.when(b == QB - 1)
    def _():
        copies = []
        for k, target in enumerate((dq0, dq1, dq2, dq3)):
            row = pl.multiple_of(((meta[AT_HEAD] + k) & (NH - 1)) * PART, PART)
            copies.append(
                pltpu.make_async_copy(dq_scr.at[pl.ds(row, PART)], target, dq_sems.at[k])
            )
        for c in copies:
            c.start()
        for c in copies:
            c.wait()


def random_kernel(
    meta, q0, q1, q2, q3, d0, d1, d2, d3, ld_ref, got_ref,
    dqt_ref, dkv_ref, q_scr, do_scr, kv_scr, out_scr, key_scr, p_scr, ds_scr, sems, in_sems, out_sems,
):
    b = pl.program_id(0)

    def fetch(e):
        return pltpu.make_async_copy(got_ref.at[meta[e] >> 4], kv_scr.at[e], in_sems.at[e])

    def give(e):
        return pltpu.make_async_copy(out_scr.at[e], dkv_ref.at[meta[e] >> 4], out_sems.at[e])

    @pl.when(b == 0)
    def _():
        for e in range(ENT):
            fetch(e).start()
        load_parts(meta, ((q0, q1, q2, q3), (d0, d1, d2, d3)), (q_scr, do_scr), sems)

    first = b * RND
    block = meta[AT_SEQ] * QB + b
    biases = []
    for j in range(RND):
        named = meta[first + j]
        r = (named >> 4) * QB + (named & 15)
        biases.append(jnp.where((r >= G) & (jnp.abs(r - block) >= 2), 0.0, MASKED))
        fetch(first + j).wait()
    lse2, delta = row_vector(ld_ref[0, 0]), row_vector(ld_ref[1, 0])
    rows = pl.ds(pl.multiple_of(b * ROWS, ROWS), ROWS)
    dk, dv, dqt = pair_grads(
        [kv_scr[first + j, 0] for j in range(RND)],
        [kv_scr[first + j, 1] for j in range(RND)],
        biases, q_scr[rows, :], do_scr[rows, :], lse2, delta, key_scr, p_scr, ds_scr,
    )
    dqt_ref[0] = dqt
    for j in range(RND):
        n = first + j
        out_scr[n, 0] = dk[j * BLK : (j + 1) * BLK].astype(BF)
        out_scr[n, 1] = dv[j * BLK : (j + 1) * BLK].astype(BF)
        give(n).start()

    @pl.when(b == QB - 1)
    def _():
        for e in range(ENT):
            give(e).wait()


def select_kernel(meta, kv_ref, out_ref):
    base = pl.program_id(0) * STEP
    for i in range(STEP):
        slot = meta[AT_WANT + base + i]

        @pl.when(slot >= 0)
        def _():
            out_ref[i] = kv_ref[slot]


def collect_kernel(meta, got, ext, lower, upper, dg, out, acc):
    step = pl.program_id(0)

    @pl.when(step == 0)
    def _():
        acc[...] = ext[1 : QB + 1]
        acc[QB - 1] += lower[0].astype(F32)
        acc[0] += upper[0].astype(F32)

        @pl.when(meta[AT_SEQ] == 0)
        def _():
            for t in range(G):
                acc[t] += dg[t]

    for i in range(STEP):
        slot = meta[AT_WANT + step * STEP + i]

        @pl.when(slot >= 0)
        def _():
            acc[slot] += got[i].astype(F32)

    @pl.when(step == NSEQ // STEP - 1)
    def _():
        out[...] = acc[...].astype(BF)


TILE = (2, BLK, HD)
PARAMS = pltpu.CompilerParams(vmem_limit_bytes=50 << 20)


def full(*shape):
    return pl.BlockSpec(shape, lambda b, m: (0,) * len(shape))


def anywhere(n):
    return [pl.BlockSpec(memory_space=ANY)] * n


def work_scratch(n):
    return [
        pltpu.VMEM((n * BLK, HD), BF),
        pltpu.VMEM((n * BLK, ROWS), BF),
        pltpu.VMEM((n * BLK, ROWS), BF),
    ]


ROW_PAIR = pl.BlockSpec((2, 1, HL, BLK), lambda b, m: (0, b, 0, 0))
DQT = pl.BlockSpec((1, HD, ROWS), lambda b, m: (b, 0, 0))


def call_near(meta, q, do, ld, kvx, gl, dqt):
    return pl.pallas_call(
        near_kernel,
        grid_spec=pltpu.PrefetchScalarGridSpec(
            num_scalar_prefetch=1,
            grid=(QB,),
            in_specs=anywhere(2 * NH) + [ROW_PAIR, full(QB + 2, *TILE), full(2 * G, BLK, HD), DQT],
            out_specs=anywhere(NH) + [full(QB + 2, *TILE), full(G, *TILE)],
            scratch_shapes=[pltpu.VMEM((QB * ROWS, HD), BF)] * 3
            + work_scratch(G + 3)
            + [pltpu.SemaphoreType.DMA((2, NH)), pltpu.SemaphoreType.DMA((NH,))],
        ),
        out_shape=[jax.ShapeDtypeStruct((PART, HD), BF)] * NH
        + [
            jax.ShapeDtypeStruct((QB + 2, *TILE), F32),
            jax.ShapeDtypeStruct((G, *TILE), F32),
        ],
        compiler_params=PARAMS,
        name="near",
    )(meta, *q, *do, ld, kvx, gl, dqt)


def call_random(meta, q, do, ld, got):
    return pl.pallas_call(
        random_kernel,
        grid_spec=pltpu.PrefetchScalarGridSpec(
            num_scalar_prefetch=1,
            grid=(QB,),
            in_specs=anywhere(2 * NH) + [ROW_PAIR] + anywhere(1),
            out_specs=[DQT] + anywhere(1),
            scratch_shapes=[pltpu.VMEM((QB * ROWS, HD), BF)] * 2
            + [pltpu.VMEM((ENT, *TILE), BF)] * 2
            + work_scratch(RND)
            + [
                pltpu.SemaphoreType.DMA((2, NH)),
                pltpu.SemaphoreType.DMA((ENT,)),
                pltpu.SemaphoreType.DMA((ENT,)),
            ],
        ),
        out_shape=[
            jax.ShapeDtypeStruct((QB, HD, ROWS), F32),
            jax.ShapeDtypeStruct((NSEQ, *TILE), BF),
        ],
        compiler_params=PARAMS,
        name="random",
    )(meta, *q, *do, ld, got)


STEP_TILES = pl.BlockSpec((STEP, *TILE), lambda b, m: (b, 0, 0, 0))


def call_select(meta, kv):
    return pl.pallas_call(
        select_kernel,
        grid_spec=pltpu.PrefetchScalarGridSpec(
            num_scalar_prefetch=1,
            grid=(NSEQ // STEP,),
            in_specs=[full(QB, *TILE)],
            out_specs=STEP_TILES,
        ),
        out_shape=jax.ShapeDtypeStruct((NSEQ, *TILE), BF),
        compiler_params=PARAMS,
        name="select",
    )(meta, kv)


def call_collect(meta, got, ext, lower, upper, dg):
    return pl.pallas_call(
        collect_kernel,
        grid_spec=pltpu.PrefetchScalarGridSpec(
            num_scalar_prefetch=1,
            grid=(NSEQ // STEP,),
            in_specs=[STEP_TILES, full(QB + 2, *TILE), full(1, *TILE), full(1, *TILE), full(G, *TILE)],
            out_specs=full(QB, *TILE),
            scratch_shapes=[pltpu.VMEM((QB, *TILE), F32)],
        ),
        out_shape=jax.ShapeDtypeStruct((QB, *TILE), BF),
        compiler_params=PARAMS,
        name="collect",
    )(meta, got, ext, lower, upper, dg)


def join_kernel(head, p0, p1, p2, p3, out):
    for k, p in enumerate((p0, p1, p2, p3)):
        out[:, (head[0] - k) & (NH - 1)] = p[...]


def call_join(head, parts):
    rows = TOK // 3
    return pl.pallas_call(
        join_kernel,
        grid_spec=pltpu.PrefetchScalarGridSpec(
            num_scalar_prefetch=1,
            grid=(3,),
            in_specs=[pl.BlockSpec((rows, HL, HD), lambda b, m: (b, 0, 0))] * NH,
            out_specs=pl.BlockSpec((rows, NH, HL, HD), lambda b, m: (b, 0, 0, 0)),
        ),
        out_shape=jax.ShapeDtypeStruct((TOK, NH, HL, HD), BF),
        name="join",
    )(head, *[p.reshape(TOK, HL, HD) for p in parts])


def plain_a2a(value, axis):
    return lax.all_to_all(value, axis, split_axis=0, concat_axis=0, tiled=True)


def turn(value, k):
    return lax.ppermute(value, "head", [(i, (i + k) % NH) for i in range(NH)]) if k else value


def head_parts(value, head):
    parts = value.reshape(TOK, NH, HL, HD)
    return [
        lax.dynamic_index_in_dim(parts, lax.rem(head + k, NH), axis=1, keepdims=False).reshape(PART, HD)
        for k in range(NH)
    ]


def tie(*values):
    return lax.optimization_barrier(values)


def spread(value, index):
    k = 1
    while k < NXC:
        got = lax.ppermute(value, ("x", "c"), [(i, i + k) for i in range(k)])
        value = jnp.where((index >= k) & (index < 2 * k), got, value)
        k *= 2
    return value


def gather_sum(value):
    k = NXC // 2
    while k:
        value = value + lax.ppermute(value, ("x", "c"), [(i + k, i) for i in range(k)])
        k //= 2
    return value


def per_device(q, k, v, o, do, lse, owner, slot):
    head, seq = lax.axis_index("head"), lax.axis_index(SEQ)
    named = (owner * 16 + slot).reshape(NSEQ, ENT)
    mine = lax.dynamic_index_in_dim(named, seq, 0, keepdims=False)
    want = jnp.max(jnp.where(named >> 4 == seq, named & 15, -1), axis=1)
    meta = jnp.concatenate([mine, jnp.stack([seq, head]).astype(jnp.int32), want])

    z, xc = lax.axis_index("z"), lax.axis_index(("x", "c"))
    up = [(i, i + 1) for i in range(NSEQ - 1)]
    down = [(i + 1, i) for i in range(NSEQ - 1)]
    kvs = jnp.stack([k, v]).transpose(2, 0, 1, 3)
    kv, meta = tie(plain_a2a(kvs, "head"), meta)
    kv = kv.transpose(1, 0, 2, 3).reshape(2, QB, BLK, HD).transpose(1, 0, 2, 3)
    got = plain_a2a(call_select(meta, kv), SEQ)

    qp, dop = head_parts(q, head), head_parts(do, head)
    ql = [turn(p, i) for i, p in enumerate(qp)]
    dol = [turn(p, i) for i, p in enumerate(dop)]
    delta = jnp.sum(do.astype(F32) * o.astype(F32), axis=-1)
    ld = jnp.stack([lse * LOG2E, delta]).reshape(2, TOK, NH, HL).transpose(2, 0, 1, 3)
    ld = ld.reshape(NH, 2, PART // BLK, BLK)
    ld = jnp.stack(
        [turn(lax.dynamic_index_in_dim(ld, lax.rem(head + i, NH), 0, keepdims=False), i) for i in range(NH)]
    )
    ld = jnp.roll(ld[::-1], head + 1, axis=0)
    ld = ld.transpose(1, 0, 2, 3).reshape(2, QB, HL, BLK)

    *parts, ld, kv = tie(*ql, *dol, ld, kv)
    ql, dol = parts[:NH], parts[NH:]
    gl = jnp.concatenate([kv[:G, 0], kv[:G, 1]])
    low = [lax.ppermute(gl, "z", [(0, i)]) for i in range(1, 4)]
    gl = jnp.where(z == 0, gl, low[0] + low[1] + low[2])
    high = lax.ppermute(gl, "z", [(i, i + 4) for i in range(4)])
    before = lax.ppermute(kv[QB - 1 :], SEQ, up)
    after = lax.ppermute(kv[:1], SEQ, down)

    dqt, back = call_random(meta, ql, dol, ld, got)
    back, before, after, high = tie(back, before, after, high)
    back = plain_a2a(back, SEQ)
    gl = spread(jnp.where(z < 4, gl, high), xc)
    kvx = jnp.concatenate([before, kv, after])
    *dq, dkvx, dg = call_near(meta, ql, dol, ld, kvx, gl, dqt)
    dq, dg = tie([turn(p, i) for i, p in enumerate(dq)], gather_sum(dg))
    dq, dg, dkvx = tie(call_join(head.reshape(1), dq), dg, dkvx)
    lower = lax.ppermute(dkvx[:1].astype(BF), SEQ, down)
    upper = lax.ppermute(dkvx[QB + 1 :].astype(BF), SEQ, up)
    part = dg.astype(BF)
    for i in range(1, NZ):
        dg = dg + lax.ppermute(part, "z", [(i, 0)]).astype(F32)
    total = call_collect(meta, back, dkvx, lower, upper, dg)
    dkv = total.transpose(1, 0, 2, 3).reshape(2, NH, TOK, HD).transpose(1, 0, 2, 3)
    dkv = plain_a2a(dkv, "head")
    dk = dkv[:, 0].transpose(1, 0, 2)
    dv = dkv[:, 1].transpose(1, 0, 2)
    return dq.reshape(TOK, NH * HL, HD), dk, dv


def solution(mesh):
    grid = Mesh(np.asarray(mesh.devices).reshape(NZ, NX, NC, NH), ("z", "x", "c", "head"))
    split = ("z", "x", "c", "head")
    wide = P(split, None, None)
    return jax.shard_map(
        per_device,
        mesh=grid,
        in_specs=(wide,) * 5 + (P(split, None), P(), P()),
        out_specs=(wide,) * 3,
        check_vma=False,
    )
```

```python
import functools

import jax
import jax.numpy as jnp
import numpy as np
from jax import lax
from jax.experimental import pallas as pl
from jax.experimental.pallas import tpu as pltpu
from jax.sharding import Mesh, PartitionSpec as P

HD = 128
BLK = 128
G = 2
RND = 3
NZ, NX, NC, NH = 8, 4, 2, 4
SEQ = ("z", "x", "c")
NXC = NX * NC
NSEQ = NZ * NXC
QB = 9
NB = NSEQ * QB
HL = 8
ROWS = BLK * HL
TOK = 288
SCALE = 1.0 / HD**0.5
LOG2E = 1.4426950408889634
MASKED = 1e30
ENT = QB * RND
AT_SEQ, AT_HEAD, AT_Z, AT_WANT = ENT, ENT + 1, ENT + 2, ENT + 3
AT_PLANE = AT_WANT + NSEQ
NEAR, FAR = (0, 1, 2, 6, 7), (3, 4, 5)
CUT = 5
STEP = 8
PART = TOK * HL
BF = jnp.bfloat16
F32 = jnp.float32
ANY = pl.ANY


def dot(a, b, ca, cb):
    return lax.dot_general(a, b, (((ca,), (cb,)), ((), ())), preferred_element_type=F32)


def row_vector(tile):
    return jnp.concatenate([tile[i : i + 1, :] for i in range(HL)], axis=1)


def pair_grads(keys, values, biases, q, do, lse2, delta, key_scr, p_scr, ds_scr):
    n = len(keys)
    for t in range(n):
        rows = pl.ds(t * BLK, BLK)
        key_scr[rows, :] = keys[t]
        s = dot(keys[t], q, 1, 1)
        p = jnp.exp2(s * (SCALE * LOG2E) - (lse2 + biases[t]))
        dp = dot(values[t], do, 1, 1)
        p_scr[rows, :] = p.astype(BF)
        ds_scr[rows, :] = (p * (dp - delta)).astype(BF)
    dv = dot(p_scr[...], do, 1, 0)
    dk = dot(ds_scr[...], q, 1, 0) * SCALE
    dqt = dot(key_scr[...], ds_scr[...], 0, 0)
    return dk, dv, dqt


def load_parts(meta, parts, whole, sems):
    copies = []
    for i, (four, target) in enumerate(zip(parts, whole)):
        for k in range(NH):
            row = pl.multiple_of(((meta[AT_HEAD] - k) & (NH - 1)) * PART, PART)
            copies.append(
                pltpu.make_async_copy(four[k], target.at[pl.ds(row, PART)], sems.at[i, k])
            )
    for c in copies:
        c.start()
    for c in copies:
        c.wait()


def near_kernel(
    meta, q0, q1, q2, q3, d0, d1, d2, d3, ld_ref, kv_ref, gl_ref, dqt_ref,
    dq0, dq1, dq2, dq3, dkv_ref, dg_ref, q_scr, do_scr, dq_scr, key_scr, p_scr, ds_scr, sems, dq_sems,
):
    b = pl.program_id(0)

    @pl.when(b == 0)
    def _():
        load_parts(meta, ((q0, q1, q2, q3), (d0, d1, d2, d3)), (q_scr, do_scr), sems)
        dkv_ref[...] = jnp.zeros_like(dkv_ref)
        dg_ref[...] = jnp.zeros_like(dg_ref)

    block = meta[AT_SEQ] * QB + b
    keys = [gl_ref[0], gl_ref[1]] + [kv_ref[b + w, 0] for w in range(3)]
    values = [gl_ref[G], gl_ref[G + 1]] + [kv_ref[b + w, 1] for w in range(3)]
    biases = [0.0, 0.0]
    for w in range(3):
        c = block + (w - 1)
        biases.append(jnp.where((c >= G) & (c <= NB - 1), 0.0, MASKED))
    lse2, delta = row_vector(ld_ref[0, 0]), row_vector(ld_ref[1, 0])
    rows = pl.ds(pl.multiple_of(b * ROWS, ROWS), ROWS)
    dk, dv, dqt = pair_grads(
        keys, values, biases, q_scr[rows, :], do_scr[rows, :], lse2, delta, key_scr, p_scr, ds_scr
    )
    dq_scr[rows, :] = ((dqt + dqt_ref[0]).T * SCALE).astype(BF)
    for t in range(G):
        dg_ref[t, 0] += dk[t * BLK : (t + 1) * BLK]
        dg_ref[t, 1] += dv[t * BLK : (t + 1) * BLK]
    for w in range(3):
        t = G + w
        dkv_ref[b + w, 0] += dk[t * BLK : (t + 1) * BLK]
        dkv_ref[b + w, 1] += dv[t * BLK : (t + 1) * BLK]

    @pl.when(b == QB - 1)
    def _():
        copies = []
        for k, target in enumerate((dq0, dq1, dq2, dq3)):
            row = pl.multiple_of(((meta[AT_HEAD] + k) & (NH - 1)) * PART, PART)
            copies.append(
                pltpu.make_async_copy(dq_scr.at[pl.ds(row, PART)], target, dq_sems.at[k])
            )
        for c in copies:
            c.start()
        for c in copies:
            c.wait()


def place_of(meta, owner):
    r = ((owner >> 3) - meta[AT_Z]) & (NZ - 1)
    far = (r >= FAR[0]) & (r <= FAR[-1])
    pos = jnp.where(r >= FAR[0], r - FAR[0], r)
    return far, (owner & (NXC - 1)) * jnp.where(far, len(FAR), len(NEAR)) + pos


def random_kernel(
    meta, q0, q1, q2, q3, d0, d1, d2, d3, ld_ref, near_ref, far_ref,
    dqt_ref, dkv_ref, q_scr, do_scr, kv_scr, out_scr, key_scr, p_scr, ds_scr, sems, in_sems, out_sems,
):
    b = pl.program_id(0)

    def fetch(src, at, e):
        return pltpu.make_async_copy(src.at[at], kv_scr.at[e], in_sems.at[e])

    def give(e):
        return pltpu.make_async_copy(out_scr.at[e], dkv_ref.at[meta[e] >> 4], out_sems.at[e])

    @pl.when(b == 0)
    def _():
        for e in range(ENT):
            far, at = place_of(meta, meta[e] >> 4)

            @pl.when(far)
            def _():
                fetch(far_ref, at, e).start()

            @pl.when(jnp.logical_not(far))
            def _():
                fetch(near_ref, at, e).start()

        load_parts(meta, ((q0, q1, q2, q3), (d0, d1, d2, d3)), (q_scr, do_scr), sems)

    first = b * RND
    block = meta[AT_SEQ] * QB + b
    biases = []
    for j in range(RND):
        named = meta[first + j]
        r = (named >> 4) * QB + (named & 15)
        biases.append(jnp.where((r >= G) & (jnp.abs(r - block) >= 2), 0.0, MASKED))
        fetch(near_ref, 0, first + j).wait()
    lse2, delta = row_vector(ld_ref[0, 0]), row_vector(ld_ref[1, 0])
    rows = pl.ds(pl.multiple_of(b * ROWS, ROWS), ROWS)
    dk, dv, dqt = pair_grads(
        [kv_scr[first + j, 0] for j in range(RND)],
        [kv_scr[first + j, 1] for j in range(RND)],
        biases, q_scr[rows, :], do_scr[rows, :], lse2, delta, key_scr, p_scr, ds_scr,
    )
    dqt_ref[0] = dqt
    for j in range(RND):
        n = first + j
        out_scr[n, 0] = dk[j * BLK : (j + 1) * BLK].astype(BF)
        out_scr[n, 1] = dv[j * BLK : (j + 1) * BLK].astype(BF)
        give(n).start()

    @pl.when(b == QB - 1)
    def _():
        for e in range(ENT):
            give(e).wait()


def select_kernel(steps, meta, *refs):
    sources, dst = refs[:-1], refs[-1]

    def lay(wanted, src, slot, at):
        @pl.when(wanted)
        def _():
            dst[at] = src[slot]

    for d in range(NXC):
        for i, r in enumerate(steps):
            slot = meta[AT_PLANE + d * NZ + r]
            at = d * len(steps) + i
            if r == 4:
                lay((slot >= 0) & (slot < CUT), sources[i], slot, at)
                lay(slot >= CUT, sources[-1], slot - CUT, at)
            else:
                lay(slot >= 0, sources[i], slot, at)


def collect_kernel(meta, got, ext, lower, upper, dg, out, acc):
    step = pl.program_id(0)

    @pl.when(step == 0)
    def _():
        acc[...] = ext[1 : QB + 1]
        acc[QB - 1] += lower[0].astype(F32)
        acc[0] += upper[0].astype(F32)

        @pl.when(meta[AT_SEQ] == 0)
        def _():
            for t in range(G):
                acc[t] += dg[t]

    for i in range(STEP):
        slot = meta[AT_WANT + step * STEP + i]

        @pl.when(slot >= 0)
        def _():
            acc[slot] += got[i].astype(F32)

    @pl.when(step == NSEQ // STEP - 1)
    def _():
        out[...] = acc[...].astype(BF)


TILE = (2, BLK, HD)
PARAMS = pltpu.CompilerParams(vmem_limit_bytes=50 << 20)


def full(*shape):
    return pl.BlockSpec(shape, lambda b, m: (0,) * len(shape))


def anywhere(n):
    return [pl.BlockSpec(memory_space=ANY)] * n


def work_scratch(n):
    return [
        pltpu.VMEM((n * BLK, HD), BF),
        pltpu.VMEM((n * BLK, ROWS), BF),
        pltpu.VMEM((n * BLK, ROWS), BF),
    ]


ROW_PAIR = pl.BlockSpec((2, 1, HL, BLK), lambda b, m: (0, b, 0, 0))
DQT = pl.BlockSpec((1, HD, ROWS), lambda b, m: (b, 0, 0))


def call_near(meta, q, do, ld, kvx, gl, dqt):
    return pl.pallas_call(
        near_kernel,
        grid_spec=pltpu.PrefetchScalarGridSpec(
            num_scalar_prefetch=1,
            grid=(QB,),
            in_specs=anywhere(2 * NH) + [ROW_PAIR, full(QB + 2, *TILE), full(2 * G, BLK, HD), DQT],
            out_specs=anywhere(NH) + [full(QB + 2, *TILE), full(G, *TILE)],
            scratch_shapes=[pltpu.VMEM((QB * ROWS, HD), BF)] * 3
            + work_scratch(G + 3)
            + [pltpu.SemaphoreType.DMA((2, NH)), pltpu.SemaphoreType.DMA((NH,))],
        ),
        out_shape=[jax.ShapeDtypeStruct((PART, HD), BF)] * NH
        + [
            jax.ShapeDtypeStruct((QB + 2, *TILE), F32),
            jax.ShapeDtypeStruct((G, *TILE), F32),
        ],
        compiler_params=PARAMS,
        name="near",
    )(meta, *q, *do, ld, kvx, gl, dqt)


def call_random(meta, q, do, ld, near, far):
    return pl.pallas_call(
        random_kernel,
        grid_spec=pltpu.PrefetchScalarGridSpec(
            num_scalar_prefetch=1,
            grid=(QB,),
            in_specs=anywhere(2 * NH) + [ROW_PAIR] + anywhere(2),
            out_specs=[DQT] + anywhere(1),
            scratch_shapes=[pltpu.VMEM((QB * ROWS, HD), BF)] * 2
            + [pltpu.VMEM((ENT, *TILE), BF)] * 2
            + work_scratch(RND)
            + [
                pltpu.SemaphoreType.DMA((2, NH)),
                pltpu.SemaphoreType.DMA((ENT,)),
                pltpu.SemaphoreType.DMA((ENT,)),
            ],
        ),
        out_shape=[
            jax.ShapeDtypeStruct((QB, HD, ROWS), F32),
            jax.ShapeDtypeStruct((NSEQ, *TILE), BF),
        ],
        compiler_params=PARAMS,
        name="random",
    )(meta, *q, *do, ld, near, far)


STEP_TILES = pl.BlockSpec((STEP, *TILE), lambda b, m: (b, 0, 0, 0))


def call_select(meta, steps, sources):
    n = NXC * len(steps)
    return pl.pallas_call(
        functools.partial(select_kernel, steps),
        grid_spec=pltpu.PrefetchScalarGridSpec(
            num_scalar_prefetch=1,
            grid=(1,),
            in_specs=[full(*x.shape) for x in sources],
            out_specs=full(n, *TILE),
        ),
        out_shape=jax.ShapeDtypeStruct((n, *TILE), BF),
        compiler_params=PARAMS,
        name="select",
    )(meta, *sources)


def call_collect(meta, got, ext, lower, upper, dg):
    return pl.pallas_call(
        collect_kernel,
        grid_spec=pltpu.PrefetchScalarGridSpec(
            num_scalar_prefetch=1,
            grid=(NSEQ // STEP,),
            in_specs=[STEP_TILES, full(QB + 2, *TILE), full(1, *TILE), full(1, *TILE), full(G, *TILE)],
            out_specs=full(QB, *TILE),
            scratch_shapes=[pltpu.VMEM((QB, *TILE), F32)],
        ),
        out_shape=jax.ShapeDtypeStruct((QB, *TILE), BF),
        compiler_params=PARAMS,
        name="collect",
    )(meta, got, ext, lower, upper, dg)


def join_kernel(head, p0, p1, p2, p3, out):
    for k, p in enumerate((p0, p1, p2, p3)):
        out[:, (head[0] - k) & (NH - 1)] = p[...]


def call_join(head, parts):
    rows = TOK // 3
    return pl.pallas_call(
        join_kernel,
        grid_spec=pltpu.PrefetchScalarGridSpec(
            num_scalar_prefetch=1,
            grid=(3,),
            in_specs=[pl.BlockSpec((rows, HL, HD), lambda b, m: (b, 0, 0))] * NH,
            out_specs=pl.BlockSpec((rows, NH, HL, HD), lambda b, m: (b, 0, 0, 0)),
        ),
        out_shape=jax.ShapeDtypeStruct((TOK, NH, HL, HD), BF),
        name="join",
    )(head, *[p.reshape(TOK, HL, HD) for p in parts])


def plain_a2a(value, axis):
    return lax.all_to_all(value, axis, split_axis=0, concat_axis=0, tiled=True)


def turn(value, k):
    return lax.ppermute(value, "head", [(i, (i + k) % NH) for i in range(NH)]) if k else value


def head_parts(value, head):
    parts = value.reshape(TOK, NH, HL, HD)
    return [
        lax.dynamic_index_in_dim(parts, lax.rem(head + k, NH), axis=1, keepdims=False).reshape(PART, HD)
        for k in range(NH)
    ]


def tie(*values):
    return lax.optimization_barrier(values)


def along_z(value, step):
    return lax.ppermute(value, "z", [(i, (i + step) % NZ) for i in range(NZ)])


def spread(value, index):
    k = 1
    while k < NXC:
        got = lax.ppermute(value, ("x", "c"), [(i, i + k) for i in range(k)])
        value = jnp.where((index >= k) & (index < 2 * k), got, value)
        k *= 2
    return value


def gather_sum(value):
    k = NXC // 2
    while k:
        value = value + lax.ppermute(value, ("x", "c"), [(i + k, i) for i in range(k)])
        k //= 2
    return value


def per_device(q, k, v, o, do, lse, owner, slot):
    head, seq = lax.axis_index("head"), lax.axis_index(SEQ)
    named = (owner * 16 + slot).reshape(NSEQ, ENT)
    mine = lax.dynamic_index_in_dim(named, seq, 0, keepdims=False)
    want = jnp.max(jnp.where(named >> 4 == seq, named & 15, -1), axis=1)
    z, xc = lax.axis_index("z"), lax.axis_index(("x", "c"))
    plane = lax.dynamic_slice_in_dim(named, z * NXC, NXC, 0)[:, None, :]
    column = ((z + jnp.arange(NZ, dtype=jnp.int32)) % NZ * NXC + xc)[None, :, None]
    ask = jnp.max(jnp.where(plane >> 4 == column, plane & 15, -1), axis=2)
    spot = jnp.stack([seq, head, z]).astype(jnp.int32)
    meta = jnp.concatenate([mine, spot, want, ask.reshape(-1)])
    up = [(i, i + 1) for i in range(NSEQ - 1)]
    down = [(i + 1, i) for i in range(NSEQ - 1)]
    delta = jnp.sum(do.astype(F32) * o.astype(F32), axis=-1)
    ld = jnp.stack([lse * LOG2E, delta]).reshape(2, TOK, NH, HL).transpose(2, 0, 1, 3)
    ld = ld.reshape(NH, 2, PART // BLK, BLK)
    lp = [lax.dynamic_index_in_dim(ld, lax.rem(head + i, NH), 0, keepdims=False) for i in range(NH)]
    qp, dop = head_parts(q, head), head_parts(do, head)

    kvs = jnp.stack([k, v]).transpose(2, 0, 1, 3)
    kv, meta, lp = tie(plain_a2a(kvs, "head"), meta, lp)
    kv = kv.transpose(1, 0, 2, 3).reshape(2, QB, BLK, HD).transpose(1, 0, 2, 3)
    u1, d1, q1, q3 = tie(along_z(kv, 1), along_z(kv, -1), turn(qp[1], 1), turn(qp[3], 3))
    u2, d2, q2 = tie(along_z(u1, 1), along_z(d1, -1), turn(qp[2], 2))
    near = plain_a2a(call_select(meta, NEAR, [kv, d1, d2, u2, u1]), ("x", "c"))
    u3, d3, do1, do3 = tie(
        along_z(u2, 1), along_z(d2, -1), turn(dop[1], 1), turn(dop[3], 3)
    )
    u4, d4, do2 = tie(along_z(u3[:CUT], 1), along_z(d3[CUT:], -1), turn(dop[2], 2))
    near, u4 = tie(near, u4)
    far, edges = tie(call_select(meta, FAR, [d3, u4, u3, d4]), kv)
    far = plain_a2a(far, ("x", "c"))
    before = lax.ppermute(edges[QB - 1 :], SEQ, up)
    after = lax.ppermute(edges[:1], SEQ, down)
    ql, dol = (qp[0], q1, q2, q3), (dop[0], do1, do2, do3)
    ld = jnp.stack([turn(p, i) for i, p in enumerate(lp)])
    ld = jnp.roll(ld[::-1], head + 1, axis=0)
    ld = ld.transpose(1, 0, 2, 3).reshape(2, QB, HL, BLK)

    dqt, back = call_random(meta, ql, dol, ld, near, far)
    gl, back, before, after = tie(kv[:G], back, before, after)
    for i, shard in enumerate((u1, u2, u3, u4, d3, d2, d1)):
        gl = jnp.where(z == i + 1, shard[:G], gl)
    gl = gl.transpose(1, 0, 2, 3).reshape(2 * G, BLK, HD)
    back = plain_a2a(back, SEQ)
    gl = spread(gl, xc)
    kvx = jnp.concatenate([before, kv, after])
    *dq, dkvx, dg = call_near(meta, ql, dol, ld, kvx, gl, dqt)
    dq, dg = tie([turn(p, i) for i, p in enumerate(dq)], gather_sum(dg))
    dq, dg, dkvx = tie(call_join(head.reshape(1), dq), dg, dkvx)
    lower = lax.ppermute(dkvx[:1].astype(BF), SEQ, down)
    upper = lax.ppermute(dkvx[QB + 1 :].astype(BF), SEQ, up)
    part = dg.astype(BF)
    for i in range(1, NZ):
        dg = dg + lax.ppermute(part, "z", [(i, 0)]).astype(F32)
    total = call_collect(meta, back, dkvx, lower, upper, dg)
    dkv = total.transpose(1, 0, 2, 3).reshape(2, NH, TOK, HD).transpose(1, 0, 2, 3)
    dkv = plain_a2a(dkv, "head")
    dk = dkv[:, 0].transpose(1, 0, 2)
    dv = dkv[:, 1].transpose(1, 0, 2)
    return dq.reshape(TOK, NH * HL, HD), dk, dv


def solution(mesh):
    grid = Mesh(np.asarray(mesh.devices).reshape(NZ, NX, NC, NH), ("z", "x", "c", "head"))
    split = ("z", "x", "c", "head")
    wide = P(split, None, None)
    return jax.shard_map(
        per_device,
        mesh=grid,
        in_specs=(wide,) * 5 + (P(split, None), P(), P()),
        out_specs=(wide,) * 3,
        check_vma=False,
    )
```

```python
import functools

import jax
import jax.numpy as jnp
import numpy as np
from jax import lax
from jax.experimental import pallas as pl
from jax.experimental.pallas import tpu as pltpu
from jax.sharding import Mesh, PartitionSpec as P

HD = 128
BLK = 128
G = 2
RND = 3
NZ, NX, NC, NH = 8, 4, 2, 4
SEQ = ("z", "x", "c")
NXC = NX * NC
NSEQ = NZ * NXC
QB = 9
NB = NSEQ * QB
HL = 8
ROWS = BLK * HL
TOK = 288
SCALE = 1.0 / HD**0.5
LOG2E = 1.4426950408889634
MASKED = 1e30
ENT = QB * RND
AT_SEQ, AT_HEAD, AT_Z, AT_WANT = ENT, ENT + 1, ENT + 2, ENT + 3
AT_PLANE = AT_WANT + NSEQ
NEAR, FAR = (0, 1, 2, 6, 7), (3, 4, 5)
CUT = 5
STEP = 8
PART = TOK * HL
BF = jnp.bfloat16
F32 = jnp.float32
ANY = pl.ANY


def dot(a, b, ca, cb):
    return lax.dot_general(a, b, (((ca,), (cb,)), ((), ())), preferred_element_type=F32)


def row_vector(tile):
    return jnp.concatenate([tile[i : i + 1, :] for i in range(HL)], axis=1)


def pair_grads(keys, values, biases, q, do, lse2, delta, key_scr, p_scr, ds_scr):
    n = len(keys)
    for t in range(n):
        rows = pl.ds(t * BLK, BLK)
        key_scr[rows, :] = keys[t]
        s = dot(keys[t], q, 1, 1)
        p = jnp.exp2(s * (SCALE * LOG2E) - (lse2 + biases[t]))
        dp = dot(values[t], do, 1, 1)
        p_scr[rows, :] = p.astype(BF)
        ds_scr[rows, :] = (p * (dp - delta)).astype(BF)
    dv = dot(p_scr[...], do, 1, 0)
    dk = dot(ds_scr[...], q, 1, 0) * SCALE
    dqt = dot(key_scr[...], ds_scr[...], 0, 0)
    return dk, dv, dqt


def load_parts(meta, parts, whole, sems):
    for k in range(NH):
        chunk = (meta[AT_HEAD] - k) & (NH - 1)
        rows = pl.ds(pl.multiple_of(chunk * PART, PART), PART)
        for i, (four, target) in enumerate(zip(parts, whole)):
            pltpu.make_async_copy(four[k], target.at[rows], sems.at[i, chunk]).start()


def await_parts(block, parts, whole, sems):
    for chunk in range(NH):

        @pl.when(block == 2 * chunk)
        def _():
            rows = pl.ds(chunk * PART, PART)
            for i, (four, target) in enumerate(zip(parts, whole)):
                pltpu.make_async_copy(four[0], target.at[rows], sems.at[i, chunk]).wait()


def near_kernel(
    meta, q0, q1, q2, q3, d0, d1, d2, d3, ld_ref, kv_ref, gl_ref, dqt_ref,
    dq0, dq1, dq2, dq3, dkv_ref, dg_ref, q_scr, do_scr, dq_scr, key_scr, p_scr, ds_scr, sems, dq_sems,
):
    b = pl.program_id(0)

    @pl.when(b == 0)
    def _():
        load_parts(meta, ((q0, q1, q2, q3), (d0, d1, d2, d3)), (q_scr, do_scr), sems)
        dkv_ref[...] = jnp.zeros_like(dkv_ref)
        dg_ref[...] = jnp.zeros_like(dg_ref)

    await_parts(b, ((q0,), (d0,)), (q_scr, do_scr), sems)

    block = meta[AT_SEQ] * QB + b
    keys = [gl_ref[0], gl_ref[1]] + [kv_ref[b + w, 0] for w in range(3)]
    values = [gl_ref[G], gl_ref[G + 1]] + [kv_ref[b + w, 1] for w in range(3)]
    biases = [0.0, 0.0]
    for w in range(3):
        c = block + (w - 1)
        biases.append(jnp.where((c >= G) & (c <= NB - 1), 0.0, MASKED))
    lse2, delta = row_vector(ld_ref[0, 0]), row_vector(ld_ref[1, 0])
    rows = pl.ds(pl.multiple_of(b * ROWS, ROWS), ROWS)
    dk, dv, dqt = pair_grads(
        keys, values, biases, q_scr[rows, :], do_scr[rows, :], lse2, delta, key_scr, p_scr, ds_scr
    )
    dq_scr[rows, :] = ((dqt + dqt_ref[0]).T * SCALE).astype(BF)
    for t in range(G):
        dg_ref[t, 0] += dk[t * BLK : (t + 1) * BLK]
        dg_ref[t, 1] += dv[t * BLK : (t + 1) * BLK]
    for w in range(3):
        t = G + w
        dkv_ref[b + w, 0] += dk[t * BLK : (t + 1) * BLK]
        dkv_ref[b + w, 1] += dv[t * BLK : (t + 1) * BLK]

    @pl.when(b == QB - 1)
    def _():
        copies = []
        for k, target in enumerate((dq0, dq1, dq2, dq3)):
            row = pl.multiple_of(((meta[AT_HEAD] + k) & (NH - 1)) * PART, PART)
            copies.append(
                pltpu.make_async_copy(dq_scr.at[pl.ds(row, PART)], target, dq_sems.at[k])
            )
        for c in copies:
            c.start()
        for c in copies:
            c.wait()


def place_of(meta, owner):
    r = ((owner >> 3) - meta[AT_Z]) & (NZ - 1)
    far = (r >= FAR[0]) & (r <= FAR[-1])
    pos = jnp.where(r >= FAR[0], r - FAR[0], r)
    return far, (owner & (NXC - 1)) * jnp.where(far, len(FAR), len(NEAR)) + pos


def random_kernel(
    meta, q0, q1, q2, q3, d0, d1, d2, d3, ld_ref, near_ref, far_ref,
    dqt_ref, dkv_ref, q_scr, do_scr, kv_scr, out_scr, key_scr, p_scr, ds_scr, sems, in_sems, out_sems,
):
    b = pl.program_id(0)

    def fetch(src, at, e):
        return pltpu.make_async_copy(src.at[at], kv_scr.at[e], in_sems.at[e])

    def give(e):
        return pltpu.make_async_copy(out_scr.at[e], dkv_ref.at[meta[e] >> 4], out_sems.at[e])

    @pl.when(b == 0)
    def _():
        for e in range(ENT):
            far, at = place_of(meta, meta[e] >> 4)

            @pl.when(far)
            def _():
                fetch(far_ref, at, e).start()

            @pl.when(jnp.logical_not(far))
            def _():
                fetch(near_ref, at, e).start()

        load_parts(meta, ((q0, q1, q2, q3), (d0, d1, d2, d3)), (q_scr, do_scr), sems)

    await_parts(b, ((q0,), (d0,)), (q_scr, do_scr), sems)
    first = b * RND
    block = meta[AT_SEQ] * QB + b
    biases = []
    for j in range(RND):
        named = meta[first + j]
        r = (named >> 4) * QB + (named & 15)
        biases.append(jnp.where((r >= G) & (jnp.abs(r - block) >= 2), 0.0, MASKED))
        fetch(near_ref, 0, first + j).wait()
    lse2, delta = row_vector(ld_ref[0, 0]), row_vector(ld_ref[1, 0])
    rows = pl.ds(pl.multiple_of(b * ROWS, ROWS), ROWS)
    dk, dv, dqt = pair_grads(
        [kv_scr[first + j, 0] for j in range(RND)],
        [kv_scr[first + j, 1] for j in range(RND)],
        biases, q_scr[rows, :], do_scr[rows, :], lse2, delta, key_scr, p_scr, ds_scr,
    )
    dqt_ref[0] = dqt
    for j in range(RND):
        n = first + j
        out_scr[n, 0] = dk[j * BLK : (j + 1) * BLK].astype(BF)
        out_scr[n, 1] = dv[j * BLK : (j + 1) * BLK].astype(BF)
        give(n).start()

    @pl.when(b == QB - 1)
    def _():
        for e in range(ENT):
            give(e).wait()


def select_kernel(steps, meta, *refs):
    sources, dst = refs[:-1], refs[-1]

    def lay(wanted, src, slot, at):
        @pl.when(wanted)
        def _():
            dst[at] = src[slot]

    for d in range(NXC):
        for i, r in enumerate(steps):
            slot = meta[AT_PLANE + d * NZ + r]
            at = d * len(steps) + i
            if r == 4:
                lay((slot >= 0) & (slot < CUT), sources[i], slot, at)
                lay(slot >= CUT, sources[-1], slot - CUT, at)
            else:
                lay(slot >= 0, sources[i], slot, at)


def collect_kernel(meta, got, ext, lower, upper, dg, out, acc):
    step = pl.program_id(0)

    @pl.when(step == 0)
    def _():
        acc[...] = ext[1 : QB + 1]
        acc[QB - 1] += lower[0].astype(F32)
        acc[0] += upper[0].astype(F32)

        @pl.when(meta[AT_SEQ] == 0)
        def _():
            for t in range(G):
                acc[t] += dg[t]

    for i in range(STEP):
        slot = meta[AT_WANT + step * STEP + i]

        @pl.when(slot >= 0)
        def _():
            acc[slot] += got[i].astype(F32)

    @pl.when(step == NSEQ // STEP - 1)
    def _():
        out[...] = acc[...].astype(BF)


TILE = (2, BLK, HD)
PARAMS = pltpu.CompilerParams(vmem_limit_bytes=50 << 20)


def full(*shape):
    return pl.BlockSpec(shape, lambda b, m: (0,) * len(shape))


def anywhere(n):
    return [pl.BlockSpec(memory_space=ANY)] * n


def work_scratch(n):
    return [
        pltpu.VMEM((n * BLK, HD), BF),
        pltpu.VMEM((n * BLK, ROWS), BF),
        pltpu.VMEM((n * BLK, ROWS), BF),
    ]


ROW_PAIR = pl.BlockSpec((2, 1, HL, BLK), lambda b, m: (0, b, 0, 0))
DQT = pl.BlockSpec((1, HD, ROWS), lambda b, m: (b, 0, 0))


def call_near(meta, q, do, ld, kvx, gl, dqt):
    return pl.pallas_call(
        near_kernel,
        grid_spec=pltpu.PrefetchScalarGridSpec(
            num_scalar_prefetch=1,
            grid=(QB,),
            in_specs=anywhere(2 * NH) + [ROW_PAIR, full(QB + 2, *TILE), full(2 * G, BLK, HD), DQT],
            out_specs=anywhere(NH) + [full(QB + 2, *TILE), full(G, *TILE)],
            scratch_shapes=[pltpu.VMEM((QB * ROWS, HD), BF)] * 3
            + work_scratch(G + 3)
            + [pltpu.SemaphoreType.DMA((2, NH)), pltpu.SemaphoreType.DMA((NH,))],
        ),
        out_shape=[jax.ShapeDtypeStruct((PART, HD), BF)] * NH
        + [
            jax.ShapeDtypeStruct((QB + 2, *TILE), F32),
            jax.ShapeDtypeStruct((G, *TILE), F32),
        ],
        compiler_params=PARAMS,
        name="near",
    )(meta, *q, *do, ld, kvx, gl, dqt)


def call_random(meta, q, do, ld, near, far):
    return pl.pallas_call(
        random_kernel,
        grid_spec=pltpu.PrefetchScalarGridSpec(
            num_scalar_prefetch=1,
            grid=(QB,),
            in_specs=anywhere(2 * NH) + [ROW_PAIR] + anywhere(2),
            out_specs=[DQT] + anywhere(1),
            scratch_shapes=[pltpu.VMEM((QB * ROWS, HD), BF)] * 2
            + [pltpu.VMEM((ENT, *TILE), BF)] * 2
            + work_scratch(RND)
            + [
                pltpu.SemaphoreType.DMA((2, NH)),
                pltpu.SemaphoreType.DMA((ENT,)),
                pltpu.SemaphoreType.DMA((ENT,)),
            ],
        ),
        out_shape=[
            jax.ShapeDtypeStruct((QB, HD, ROWS), F32),
            jax.ShapeDtypeStruct((NSEQ, *TILE), BF),
        ],
        compiler_params=PARAMS,
        name="random",
    )(meta, *q, *do, ld, near, far)


STEP_TILES = pl.BlockSpec((STEP, *TILE), lambda b, m: (b, 0, 0, 0))


def call_select(meta, steps, sources):
    n = NXC * len(steps)
    return pl.pallas_call(
        functools.partial(select_kernel, steps),
        grid_spec=pltpu.PrefetchScalarGridSpec(
            num_scalar_prefetch=1,
            grid=(1,),
            in_specs=[full(*x.shape) for x in sources],
            out_specs=full(n, *TILE),
        ),
        out_shape=jax.ShapeDtypeStruct((n, *TILE), BF),
        compiler_params=PARAMS,
        name="select",
    )(meta, *sources)


def call_collect(meta, got, ext, lower, upper, dg):
    return pl.pallas_call(
        collect_kernel,
        grid_spec=pltpu.PrefetchScalarGridSpec(
            num_scalar_prefetch=1,
            grid=(NSEQ // STEP,),
            in_specs=[STEP_TILES, full(QB + 2, *TILE), full(1, *TILE), full(1, *TILE), full(G, *TILE)],
            out_specs=full(QB, *TILE),
            scratch_shapes=[pltpu.VMEM((QB, *TILE), F32)],
        ),
        out_shape=jax.ShapeDtypeStruct((QB, *TILE), BF),
        compiler_params=PARAMS,
        name="collect",
    )(meta, got, ext, lower, upper, dg)


def join_kernel(head, p0, p1, p2, p3, out):
    for k, p in enumerate((p0, p1, p2, p3)):
        out[:, (head[0] - k) & (NH - 1)] = p[...]


def call_join(head, parts):
    rows = TOK // 3
    return pl.pallas_call(
        join_kernel,
        grid_spec=pltpu.PrefetchScalarGridSpec(
            num_scalar_prefetch=1,
            grid=(3,),
            in_specs=[pl.BlockSpec((rows, HL, HD), lambda b, m: (b, 0, 0))] * NH,
            out_specs=pl.BlockSpec((rows, NH, HL, HD), lambda b, m: (b, 0, 0, 0)),
        ),
        out_shape=jax.ShapeDtypeStruct((TOK, NH, HL, HD), BF),
        name="join",
    )(head, *[p.reshape(TOK, HL, HD) for p in parts])


def plain_a2a(value, axis):
    return lax.all_to_all(value, axis, split_axis=0, concat_axis=0, tiled=True)


def turn(value, k):
    return lax.ppermute(value, "head", [(i, (i + k) % NH) for i in range(NH)]) if k else value


def head_parts(value, head):
    parts = value.reshape(TOK, NH, HL, HD)
    return [
        lax.dynamic_index_in_dim(parts, lax.rem(head + k, NH), axis=1, keepdims=False).reshape(PART, HD)
        for k in range(NH)
    ]


def tie(*values):
    return lax.optimization_barrier(values)


def along_z(value, step):
    return lax.ppermute(value, "z", [(i, (i + step) % NZ) for i in range(NZ)])


def spread(value, index):
    k = 1
    while k < NXC:
        got = lax.ppermute(value, ("x", "c"), [(i, i + k) for i in range(k)])
        value = jnp.where((index >= k) & (index < 2 * k), got, value)
        k *= 2
    return value


def gather_sum(value):
    k = NXC // 2
    while k:
        value = value + lax.ppermute(value, ("x", "c"), [(i + k, i) for i in range(k)])
        k //= 2
    return value


def per_device(q, k, v, o, do, lse, owner, slot):
    head, seq = lax.axis_index("head"), lax.axis_index(SEQ)
    named = (owner * 16 + slot).reshape(NSEQ, ENT)
    mine = lax.dynamic_index_in_dim(named, seq, 0, keepdims=False)
    want = jnp.max(jnp.where(named >> 4 == seq, named & 15, -1), axis=1)
    z, xc = lax.axis_index("z"), lax.axis_index(("x", "c"))
    plane = lax.dynamic_slice_in_dim(named, z * NXC, NXC, 0)[:, None, :]
    column = ((z + jnp.arange(NZ, dtype=jnp.int32)) % NZ * NXC + xc)[None, :, None]
    ask = jnp.max(jnp.where(plane >> 4 == column, plane & 15, -1), axis=2)
    spot = jnp.stack([seq, head, z]).astype(jnp.int32)
    meta = jnp.concatenate([mine, spot, want, ask.reshape(-1)])
    up = [(i, i + 1) for i in range(NSEQ - 1)]
    down = [(i + 1, i) for i in range(NSEQ - 1)]
    delta = jnp.sum(do.astype(F32) * o.astype(F32), axis=-1)
    ld = jnp.stack([lse * LOG2E, delta]).reshape(2, TOK, NH, HL).transpose(2, 0, 1, 3)
    ld = ld.reshape(NH, 2, PART // BLK, BLK)
    lp = [lax.dynamic_index_in_dim(ld, lax.rem(head + i, NH), 0, keepdims=False) for i in range(NH)]
    qp, dop = head_parts(q, head), head_parts(do, head)

    kvs = jnp.stack([k, v]).transpose(2, 0, 1, 3)
    kv, meta, lp = tie(plain_a2a(kvs, "head"), meta, lp)
    kv = kv.transpose(1, 0, 2, 3).reshape(2, QB, BLK, HD).transpose(1, 0, 2, 3)
    u1, d1, q1, q3 = tie(along_z(kv, 1), along_z(kv, -1), turn(qp[1], 1), turn(qp[3], 3))
    u2, d2, q2 = tie(along_z(u1, 1), along_z(d1, -1), turn(qp[2], 2))
    near = plain_a2a(call_select(meta, NEAR, [kv, d1, d2, u2, u1]), ("x", "c"))
    u3, d3, do1, do3 = tie(
        along_z(u2, 1), along_z(d2, -1), turn(dop[1], 1), turn(dop[3], 3)
    )
    u4, d4, do2 = tie(along_z(u3[:CUT], 1), along_z(d3[CUT:], -1), turn(dop[2], 2))
    near, u4 = tie(near, u4)
    far, edges = tie(call_select(meta, FAR, [d3, u4, u3, d4]), kv)
    far = plain_a2a(far, ("x", "c"))
    before = lax.ppermute(edges[QB - 1 :], SEQ, up)
    after = lax.ppermute(edges[:1], SEQ, down)
    ql, dol = (qp[0], q1, q2, q3), (dop[0], do1, do2, do3)
    ld = jnp.stack([turn(p, i) for i, p in enumerate(lp)])
    ld = jnp.roll(ld[::-1], head + 1, axis=0)
    ld = ld.transpose(1, 0, 2, 3).reshape(2, QB, HL, BLK)

    dqt, back = call_random(meta, ql, dol, ld, near, far)
    gl, back, before, after = tie(kv[:G], back, before, after)
    for i, shard in enumerate((u1, u2, u3, u4, d3, d2, d1)):
        gl = jnp.where(z == i + 1, shard[:G], gl)
    gl = gl.transpose(1, 0, 2, 3).reshape(2 * G, BLK, HD)
    back = plain_a2a(back, SEQ)
    gl = spread(gl, xc)
    kvx = jnp.concatenate([before, kv, after])
    *dq, dkvx, dg = call_near(meta, ql, dol, ld, kvx, gl, dqt)
    dq, dg = tie([turn(p, i) for i, p in enumerate(dq)], gather_sum(dg))
    dq, dg, dkvx = tie(call_join(head.reshape(1), dq), dg, dkvx)
    lower = lax.ppermute(dkvx[:1].astype(BF), SEQ, down)
    upper = lax.ppermute(dkvx[QB + 1 :].astype(BF), SEQ, up)
    half = lax.ppermute(dg.astype(BF), "z", [(i + 4, i) for i in range(4)])
    half, lower, upper = tie(half, lower, upper)
    dg = dg + half.astype(F32)
    part = dg.astype(BF)
    for some in [lax.ppermute(part, "z", [(i, 0)]) for i in range(1, 4)]:
        dg = dg + some.astype(F32)
    total = call_collect(meta, back, dkvx, lower, upper, dg)
    dkv = total.transpose(1, 0, 2, 3).reshape(2, NH, TOK, HD).transpose(1, 0, 2, 3)
    dkv = plain_a2a(dkv, "head")
    dk = dkv[:, 0].transpose(1, 0, 2)
    dv = dkv[:, 1].transpose(1, 0, 2)
    return dq.reshape(TOK, NH * HL, HD), dk, dv


def solution(mesh):
    grid = Mesh(np.asarray(mesh.devices).reshape(NZ, NX, NC, NH), ("z", "x", "c", "head"))
    split = ("z", "x", "c", "head")
    wide = P(split, None, None)
    return jax.shard_map(
        per_device,
        mesh=grid,
        in_specs=(wide,) * 5 + (P(split, None), P(), P()),
        out_specs=(wide,) * 3,
        check_vma=False,
    )
```

```python
import functools

import jax
import jax.numpy as jnp
import numpy as np
from jax import lax
from jax.experimental import pallas as pl
from jax.experimental.pallas import tpu as pltpu
from jax.sharding import Mesh, PartitionSpec as P

HD = 128
BLK = 128
G = 2
RND = 3
NZ, NX, NC, NH = 8, 4, 2, 4
SEQ = ("z", "x", "c")
NXC = NX * NC
NSEQ = NZ * NXC
QB = 9
NB = NSEQ * QB
HL = 8
ROWS = BLK * HL
TOK = 288
SCALE = 1.0 / HD**0.5
LOG2E = 1.4426950408889634
MASKED = 1e30
ENT = QB * RND
AT_SEQ, AT_HEAD, AT_Z, AT_WANT = ENT, ENT + 1, ENT + 2, ENT + 3
AT_PLANE = AT_WANT + NSEQ
NEAR, FAR = (0, 1, 2, 6, 7), (3, 4, 5)
CUT = 5
STEP = 8
PART = TOK * HL
BF = jnp.bfloat16
F32 = jnp.float32
ANY = pl.ANY


def dot(a, b, ca, cb):
    return lax.dot_general(a, b, (((ca,), (cb,)), ((), ())), preferred_element_type=F32)


def row_vector(tile):
    return jnp.concatenate([tile[i : i + 1, :] for i in range(HL)], axis=1)


def pair_grads(keys, values, biases, q, do, lse2, delta, key_scr, p_scr, ds_scr):
    n = len(keys)
    for t in range(n):
        rows = pl.ds(t * BLK, BLK)
        key_scr[rows, :] = keys[t]
        s = dot(keys[t], q, 1, 1)
        p = jnp.exp2(s * (SCALE * LOG2E) - (lse2 + biases[t]))
        dp = dot(values[t], do, 1, 1)
        p_scr[rows, :] = p.astype(BF)
        ds_scr[rows, :] = (p * (dp - delta)).astype(BF)
    dv = dot(p_scr[...], do, 1, 0)
    dk = dot(ds_scr[...], q, 1, 0) * SCALE
    dqt = dot(key_scr[...], ds_scr[...], 0, 0)
    return dk, dv, dqt


def load_parts(meta, parts, whole, sems):
    for k in range(NH):
        chunk = (meta[AT_HEAD] - k) & (NH - 1)
        rows = pl.ds(pl.multiple_of(chunk * PART, PART), PART)
        for i, (four, target) in enumerate(zip(parts, whole)):
            pltpu.make_async_copy(four[k], target.at[rows], sems.at[i, chunk]).start()


def await_parts(block, parts, whole, sems):
    for chunk in range(NH):

        @pl.when(block == 2 * chunk)
        def _():
            rows = pl.ds(chunk * PART, PART)
            for i, (four, target) in enumerate(zip(parts, whole)):
                pltpu.make_async_copy(four[0], target.at[rows], sems.at[i, chunk]).wait()


def near_kernel(
    meta, q0, q1, q2, q3, d0, d1, d2, d3, ld_ref, kv_ref, gl_ref, dqt_ref,
    dq0, dq1, dq2, dq3, dkv_ref, dg_ref, q_scr, do_scr, dq_scr, key_scr, p_scr, ds_scr, sems, dq_sems,
):
    b = pl.program_id(0)

    @pl.when(b == 0)
    def _():
        load_parts(meta, ((q0, q1, q2, q3), (d0, d1, d2, d3)), (q_scr, do_scr), sems)
        dkv_ref[...] = jnp.zeros_like(dkv_ref)
        dg_ref[...] = jnp.zeros_like(dg_ref)

    await_parts(b, ((q0,), (d0,)), (q_scr, do_scr), sems)

    block = meta[AT_SEQ] * QB + b
    keys = [gl_ref[0], gl_ref[1]] + [kv_ref[b + w, 0] for w in range(3)]
    values = [gl_ref[G], gl_ref[G + 1]] + [kv_ref[b + w, 1] for w in range(3)]
    biases = [0.0, 0.0]
    for w in range(3):
        c = block + (w - 1)
        biases.append(jnp.where((c >= G) & (c <= NB - 1), 0.0, MASKED))
    lse2, delta = row_vector(ld_ref[0, 0]), row_vector(ld_ref[1, 0])
    rows = pl.ds(pl.multiple_of(b * ROWS, ROWS), ROWS)
    dk, dv, dqt = pair_grads(
        keys, values, biases, q_scr[rows, :], do_scr[rows, :], lse2, delta, key_scr, p_scr, ds_scr
    )
    dq_scr[rows, :] = ((dqt + dqt_ref[0]).T * SCALE).astype(BF)
    for t in range(G):
        dg_ref[t, 0] += dk[t * BLK : (t + 1) * BLK]
        dg_ref[t, 1] += dv[t * BLK : (t + 1) * BLK]
    for w in range(3):
        t = G + w
        dkv_ref[b + w, 0] += dk[t * BLK : (t + 1) * BLK]
        dkv_ref[b + w, 1] += dv[t * BLK : (t + 1) * BLK]

    @pl.when(b == QB - 1)
    def _():
        copies = []
        for k, target in enumerate((dq0, dq1, dq2, dq3)):
            row = pl.multiple_of(((meta[AT_HEAD] + k) & (NH - 1)) * PART, PART)
            copies.append(
                pltpu.make_async_copy(dq_scr.at[pl.ds(row, PART)], target, dq_sems.at[k])
            )
        for c in copies:
            c.start()
        for c in copies:
            c.wait()


def place_of(meta, owner):
    r = ((owner >> 3) - meta[AT_Z]) & (NZ - 1)
    far = (r >= FAR[0]) & (r <= FAR[-1])
    pos = jnp.where(r >= FAR[0], r - FAR[0], r)
    return far, (owner & (NXC - 1)) * jnp.where(far, len(FAR), len(NEAR)) + pos


def random_kernel(
    meta, q0, q1, q2, q3, d0, d1, d2, d3, ld_ref, near_ref, far_ref,
    dqt_ref, dkv_ref, q_scr, do_scr, kv_scr, out_scr, key_scr, p_scr, ds_scr, sems, in_sems, out_sems,
):
    b = pl.program_id(0)

    def fetch(src, at, e):
        return pltpu.make_async_copy(src.at[at], kv_scr.at[e], in_sems.at[e])

    def give(e):
        return pltpu.make_async_copy(out_scr.at[e], dkv_ref.at[meta[e] >> 4], out_sems.at[e])

    @pl.when(b == 0)
    def _():
        for e in range(ENT):
            far, at = place_of(meta, meta[e] >> 4)

            @pl.when(far)
            def _():
                fetch(far_ref, at, e).start()

            @pl.when(jnp.logical_not(far))
            def _():
                fetch(near_ref, at, e).start()

        load_parts(meta, ((q0, q1, q2, q3), (d0, d1, d2, d3)), (q_scr, do_scr), sems)

    await_parts(b, ((q0,), (d0,)), (q_scr, do_scr), sems)
    first = b * RND
    block = meta[AT_SEQ] * QB + b
    biases = []
    for j in range(RND):
        named = meta[first + j]
        r = (named >> 4) * QB + (named & 15)
        biases.append(jnp.where((r >= G) & (jnp.abs(r - block) >= 2), 0.0, MASKED))
        fetch(near_ref, 0, first + j).wait()
    lse2, delta = row_vector(ld_ref[0, 0]), row_vector(ld_ref[1, 0])
    rows = pl.ds(pl.multiple_of(b * ROWS, ROWS), ROWS)
    dk, dv, dqt = pair_grads(
        [kv_scr[first + j, 0] for j in range(RND)],
        [kv_scr[first + j, 1] for j in range(RND)],
        biases, q_scr[rows, :], do_scr[rows, :], lse2, delta, key_scr, p_scr, ds_scr,
    )
    dqt_ref[0] = dqt
    for j in range(RND):
        n = first + j
        out_scr[n, 0] = dk[j * BLK : (j + 1) * BLK].astype(BF)
        out_scr[n, 1] = dv[j * BLK : (j + 1) * BLK].astype(BF)
        give(n).start()

    @pl.when(b == QB - 1)
    def _():
        for e in range(ENT):
            give(e).wait()


def select_kernel(steps, meta, *refs):
    sources, dst = refs[:-1], refs[-1]

    def lay(wanted, src, slot, at):
        @pl.when(wanted)
        def _():
            dst[at] = src[slot]

    for d in range(NXC):
        for i, r in enumerate(steps):
            slot = meta[AT_PLANE + d * NZ + r]
            at = d * len(steps) + i
            if r == 4:
                lay((slot >= 0) & (slot < CUT), sources[i], slot, at)
                lay(slot >= CUT, sources[-1], slot - CUT, at)
            else:
                lay(slot >= 0, sources[i], slot, at)


def collect_kernel(meta, got, ext, lower, upper, dg, out, acc):
    step = pl.program_id(0)

    @pl.when(step == 0)
    def _():
        acc[...] = ext[1 : QB + 1]
        acc[QB - 1] += lower[0].astype(F32)
        acc[0] += upper[0].astype(F32)

        @pl.when(meta[AT_SEQ] == 0)
        def _():
            for t in range(G):
                acc[t] += dg[t]

    for i in range(STEP):
        slot = meta[AT_WANT + step * STEP + i]

        @pl.when(slot >= 0)
        def _():
            acc[slot] += got[i].astype(F32)

    @pl.when(step == NSEQ // STEP - 1)
    def _():
        out[...] = acc[...].astype(BF)


TILE = (2, BLK, HD)
PARAMS = pltpu.CompilerParams(vmem_limit_bytes=50 << 20)


def full(*shape):
    return pl.BlockSpec(shape, lambda b, m: (0,) * len(shape))


def anywhere(n):
    return [pl.BlockSpec(memory_space=ANY)] * n


def work_scratch(n):
    return [
        pltpu.VMEM((n * BLK, HD), BF),
        pltpu.VMEM((n * BLK, ROWS), BF),
        pltpu.VMEM((n * BLK, ROWS), BF),
    ]


ROW_PAIR = pl.BlockSpec((2, 1, HL, BLK), lambda b, m: (0, b, 0, 0))
DQT = pl.BlockSpec((1, HD, ROWS), lambda b, m: (b, 0, 0))


def call_near(meta, q, do, ld, kvx, gl, dqt):
    return pl.pallas_call(
        near_kernel,
        grid_spec=pltpu.PrefetchScalarGridSpec(
            num_scalar_prefetch=1,
            grid=(QB,),
            in_specs=anywhere(2 * NH) + [ROW_PAIR, full(QB + 2, *TILE), full(2 * G, BLK, HD), DQT],
            out_specs=anywhere(NH) + [full(QB + 2, *TILE), full(G, *TILE)],
            scratch_shapes=[pltpu.VMEM((QB * ROWS, HD), BF)] * 3
            + work_scratch(G + 3)
            + [pltpu.SemaphoreType.DMA((2, NH)), pltpu.SemaphoreType.DMA((NH,))],
        ),
        out_shape=[jax.ShapeDtypeStruct((PART, HD), BF)] * NH
        + [
            jax.ShapeDtypeStruct((QB + 2, *TILE), F32),
            jax.ShapeDtypeStruct((G, *TILE), F32),
        ],
        compiler_params=PARAMS,
        name="near",
    )(meta, *q, *do, ld, kvx, gl, dqt)


def call_random(meta, q, do, ld, near, far):
    return pl.pallas_call(
        random_kernel,
        grid_spec=pltpu.PrefetchScalarGridSpec(
            num_scalar_prefetch=1,
            grid=(QB,),
            in_specs=anywhere(2 * NH) + [ROW_PAIR] + anywhere(2),
            out_specs=[DQT] + anywhere(1),
            scratch_shapes=[pltpu.VMEM((QB * ROWS, HD), BF)] * 2
            + [pltpu.VMEM((ENT, *TILE), BF)] * 2
            + work_scratch(RND)
            + [
                pltpu.SemaphoreType.DMA((2, NH)),
                pltpu.SemaphoreType.DMA((ENT,)),
                pltpu.SemaphoreType.DMA((ENT,)),
            ],
        ),
        out_shape=[
            jax.ShapeDtypeStruct((QB, HD, ROWS), F32),
            jax.ShapeDtypeStruct((NSEQ, *TILE), BF),
        ],
        compiler_params=PARAMS,
        name="random",
    )(meta, *q, *do, ld, near, far)


STEP_TILES = pl.BlockSpec((STEP, *TILE), lambda b, m: (b, 0, 0, 0))


def call_select(meta, steps, sources):
    n = NXC * len(steps)
    return pl.pallas_call(
        functools.partial(select_kernel, steps),
        grid_spec=pltpu.PrefetchScalarGridSpec(
            num_scalar_prefetch=1,
            grid=(1,),
            in_specs=[full(*x.shape) for x in sources],
            out_specs=full(n, *TILE),
        ),
        out_shape=jax.ShapeDtypeStruct((n, *TILE), BF),
        compiler_params=PARAMS,
        name="select",
    )(meta, *sources)


def call_collect(meta, got, ext, lower, upper, dg):
    return pl.pallas_call(
        collect_kernel,
        grid_spec=pltpu.PrefetchScalarGridSpec(
            num_scalar_prefetch=1,
            grid=(NSEQ // STEP,),
            in_specs=[STEP_TILES, full(QB + 2, *TILE), full(1, *TILE), full(1, *TILE), full(G, *TILE)],
            out_specs=full(QB, *TILE),
            scratch_shapes=[pltpu.VMEM((QB, *TILE), F32)],
        ),
        out_shape=jax.ShapeDtypeStruct((QB, *TILE), BF),
        compiler_params=PARAMS,
        name="collect",
    )(meta, got, ext, lower, upper, dg)


def join_kernel(head, p0, p1, p2, p3, out):
    for k, p in enumerate((p0, p1, p2, p3)):
        out[:, (head[0] - k) & (NH - 1)] = p[...]


def call_join(head, parts):
    rows = TOK // 3
    return pl.pallas_call(
        join_kernel,
        grid_spec=pltpu.PrefetchScalarGridSpec(
            num_scalar_prefetch=1,
            grid=(3,),
            in_specs=[pl.BlockSpec((rows, HL, HD), lambda b, m: (b, 0, 0))] * NH,
            out_specs=pl.BlockSpec((rows, NH, HL, HD), lambda b, m: (b, 0, 0, 0)),
        ),
        out_shape=jax.ShapeDtypeStruct((TOK, NH, HL, HD), BF),
        name="join",
    )(head, *[p.reshape(TOK, HL, HD) for p in parts])


def plain_a2a(value, axis):
    return lax.all_to_all(value, axis, split_axis=0, concat_axis=0, tiled=True)


def turn(value, k):
    return lax.ppermute(value, "head", [(i, (i + k) % NH) for i in range(NH)]) if k else value


def head_parts(value, head):
    parts = value.reshape(TOK, NH, HL, HD)
    return [
        lax.dynamic_index_in_dim(parts, lax.rem(head + k, NH), axis=1, keepdims=False).reshape(PART, HD)
        for k in range(NH)
    ]


def tie(*values):
    return lax.optimization_barrier(values)


def along_z(value, step):
    return lax.ppermute(value, "z", [(i, (i + step) % NZ) for i in range(NZ)])


def spread(value, index):
    k = 1
    while k < NXC:
        got = lax.ppermute(value, ("x", "c"), [(i, i + k) for i in range(k)])
        value = jnp.where((index >= k) & (index < 2 * k), got, value)
        k *= 2
    return value


def gather_sum(value):
    k = NXC // 2
    while k:
        value = value + lax.ppermute(value, ("x", "c"), [(i + k, i) for i in range(k)])
        k //= 2
    return value


def per_device(q, k, v, o, do, lse, owner, slot):
    head, seq = lax.axis_index("head"), lax.axis_index(SEQ)
    named = (owner * 16 + slot).reshape(NSEQ, ENT)
    mine = lax.dynamic_index_in_dim(named, seq, 0, keepdims=False)
    want = jnp.max(jnp.where(named >> 4 == seq, named & 15, -1), axis=1)
    z, xc = lax.axis_index("z"), lax.axis_index(("x", "c"))
    plane = lax.dynamic_slice_in_dim(named, z * NXC, NXC, 0)[:, None, :]
    column = ((z + jnp.arange(NZ, dtype=jnp.int32)) % NZ * NXC + xc)[None, :, None]
    ask = jnp.max(jnp.where(plane >> 4 == column, plane & 15, -1), axis=2)
    spot = jnp.stack([seq, head, z]).astype(jnp.int32)
    meta = jnp.concatenate([mine, spot, want, ask.reshape(-1)])
    up = [(i, i + 1) for i in range(NSEQ - 1)]
    down = [(i + 1, i) for i in range(NSEQ - 1)]
    delta = jnp.sum(do.astype(F32) * o.astype(F32), axis=-1)
    ld = jnp.stack([lse * LOG2E, delta]).reshape(2, TOK, NH, HL).transpose(2, 0, 1, 3)
    ld = ld.reshape(NH, 2, PART // BLK, BLK)
    lp = [lax.dynamic_index_in_dim(ld, lax.rem(head + i, NH), 0, keepdims=False) for i in range(NH)]
    qp, dop = head_parts(q, head), head_parts(do, head)

    kvs = jnp.stack([k, v]).transpose(2, 0, 1, 3)
    kv, meta, lp = tie(plain_a2a(kvs, "head"), meta, lp)
    kv = kv.transpose(1, 0, 2, 3).reshape(2, QB, BLK, HD).transpose(1, 0, 2, 3)
    u1, d1, q1, q3, lp[1] = tie(
        along_z(kv, 1), along_z(kv, -1), turn(qp[1], 1), turn(qp[3], 3), turn(lp[1], 1)
    )
    u2, d2, q2, lp[2], lp[3] = tie(
        along_z(u1, 1), along_z(d1, -1), turn(qp[2], 2), turn(lp[2], 2), turn(lp[3], 3)
    )
    near = plain_a2a(call_select(meta, NEAR, [kv, d1, d2, u2, u1]), ("x", "c"))
    u3, d3, do1, do3 = tie(
        along_z(u2, 1), along_z(d2, -1), turn(dop[1], 1), turn(dop[3], 3)
    )
    ld = jnp.roll(jnp.stack(lp[::-1]), head + 1, axis=0)
    ld = ld.transpose(1, 0, 2, 3).reshape(2, QB, HL, BLK)
    u4, d4, do2, ld = tie(along_z(u3[:CUT], 1), along_z(d3[CUT:], -1), turn(dop[2], 2), ld)
    near, u4 = tie(near, u4)
    far, edges = tie(call_select(meta, FAR, [d3, u4, u3, d4]), kv)
    far = plain_a2a(far, ("x", "c"))
    before = lax.ppermute(edges[QB - 1 :], SEQ, up)
    after = lax.ppermute(edges[:1], SEQ, down)
    ql, dol = (qp[0], q1, q2, q3), (dop[0], do1, do2, do3)

    dqt, back = call_random(meta, ql, dol, ld, near, far)
    gl, back, before, after = tie(kv[:G], back, before, after)
    for i, shard in enumerate((u1, u2, u3, u4, d3, d2, d1)):
        gl = jnp.where(z == i + 1, shard[:G], gl)
    gl = gl.transpose(1, 0, 2, 3).reshape(2 * G, BLK, HD)
    back = plain_a2a(back, SEQ)
    gl = spread(gl, xc)
    kvx = jnp.concatenate([before, kv, after])
    *dq, dkvx, dg = call_near(meta, ql, dol, ld, kvx, gl, dqt)
    dq, dg = tie([turn(p, i) for i, p in enumerate(dq)], gather_sum(dg))
    dq, dg, dkvx = tie(call_join(head.reshape(1), dq), dg, dkvx)
    lower = lax.ppermute(dkvx[:1].astype(BF), SEQ, down)
    upper = lax.ppermute(dkvx[QB + 1 :].astype(BF), SEQ, up)
    half = lax.ppermute(dg.astype(BF), "z", [(i + 4, i) for i in range(4)])
    half, lower, upper = tie(half, lower, upper)
    dg = dg + half.astype(F32)
    part = dg.astype(BF)
    for some in [lax.ppermute(part, "z", [(i, 0)]) for i in range(1, 4)]:
        dg = dg + some.astype(F32)
    total = call_collect(meta, back, dkvx, lower, upper, dg)
    dkv = total.transpose(1, 0, 2, 3).reshape(2, NH, TOK, HD).transpose(1, 0, 2, 3)
    dkv = plain_a2a(dkv, "head")
    dk = dkv[:, 0].transpose(1, 0, 2)
    dv = dkv[:, 1].transpose(1, 0, 2)
    return dq.reshape(TOK, NH * HL, HD), dk, dv


def solution(mesh):
    grid = Mesh(np.asarray(mesh.devices).reshape(NZ, NX, NC, NH), ("z", "x", "c", "head"))
    split = ("z", "x", "c", "head")
    wide = P(split, None, None)
    return jax.shard_map(
        per_device,
        mesh=grid,
        in_specs=(wide,) * 5 + (P(split, None), P(), P()),
        out_specs=(wide,) * 3,
        check_vma=False,
    )
```
